128 devices in a mesh: freq: 4 (over z), tile: 32 (over x, y, core).
Axes of the slice: x: 4, y: 4, z: 4, core: 2. Of those that a mesh axis runs over, the one named last changes fastest.
Arguments:
- data_vec: float32 [2, 64, 4, 2048], P(None, 'freq', None, 'tile'), may hold values from -40 to 40
- direction: float32 [2, 64, 4, 15360], P(None, 'freq', None, 'tile'), may hold values from -40 to 40
- model: float32 [2, 64, 4, 15360], P(None, 'freq', None, 'tile'), may hold values from -6 to 6
- alpha: float32 [], replicated, may hold values from 0.5 to 2
- u_factor: bfloat16 [64, 480, 2, 48, 256], P('freq', 'tile'), may hold values from -0.125 to 0.125
- v_factor: bfloat16 [64, 480, 2, 48, 256], P('freq', 'tile'), may hold values from -0.375 to 0.375
- ranks: int32 [64, 480], P('freq', 'tile'), may hold values from 16 to 48
- tile_source_block: int32 [480], P('tile'), may hold values from 0 to 7, as said below
- tile_receiver_block: int32 [480], P('tile'), may hold values from 0 to 59
- time_lo: int32 [15360], P('tile'), may hold values from 0 to 255
- time_len: int32 [15360], P('tile'), may hold values from 128 to 256
Outputs:
- u_next: float32 [2, 64, 4, 2048], P(None, 'freq', None, 'tile')
- v_next: float32 [2, 64, 4, 15360], P(None, 'freq', None, 'tile')
- model_next: float32 [2, 64, 4, 15360], P(None, 'freq', None, 'tile')
The draws below stay inside these ranges and needn't reach their ends.
Inputs may be any that keep to these rules, and one draw needn't show every extreme that they name: tile_source_block and tile_receiver_block together name each tile of the 8 x 60 grid exactly once, in the order of a Hilbert curve over the grid placed in the smallest power-of-two square that holds it (cells outside the grid skipped), with the grid's rows, its columns or both possibly reversed first and the start of the order moved cyclically by any number of slots; a device's slots are consecutive in that order.
All inputs are finite; a program needn't handle non-finite values.
Results may differ from the reference program's by a relative error of at most 0.0038.
Values may be sent and summed in bfloat16 or wider, within the bound.
No kernel may reach another device: no remote copies, remote signals or barrier semaphores. Data moves between devices by JAX's collectives and lax.ppermute only.
A program may use at most 192 MiB of HBM per device.

```python
import math
import jax
import jax.numpy as jnp
from jax import lax

WINDOW_FREQS = 64
NT = 512
FLO = 8
TILE_EXTENT = 256
RMAX = 48
RLO = 16
RECEIVER_BLOCKS = 60
NVS = 4
R = 15360
TILES = 480
NRB = 8
S = 2048


def curve_cells(key):
    total = NRB * RECEIVER_BLOCKS
    side = 1
    while side < max(NRB, RECEIVER_BLOCKS):
        side = side * 2
    first_key, second_key, third_key = jax.random.split(key, 3)
    flip_rows = jax.random.randint(first_key, (), 0, 2)
    flip_cols = jax.random.randint(second_key, (), 0, 2)
    offset = jax.random.randint(third_key, (), 0, total)
    index = jnp.arange(total, dtype=jnp.int32)
    row = index // RECEIVER_BLOCKS
    col = index % RECEIVER_BLOCKS
    ypos = jnp.where(flip_rows == 1, NRB - 1 - row, row)
    xpos = jnp.where(flip_cols == 1, RECEIVER_BLOCKS - 1 - col, col)
    curve = jnp.zeros((total,), jnp.int32)
    level = side // 2
    while level > 0:
        right_half = (xpos & level > 0).astype(jnp.int32)
        upper_half = (ypos & level > 0).astype(jnp.int32)
        curve = curve + level * level * (3 * right_half ^ upper_half)
        flipped = (upper_half == 0) & (right_half == 1)
        xpos = jnp.where(flipped, side - 1 - xpos, xpos)
        ypos = jnp.where(flipped, side - 1 - ypos, ypos)
        turned = upper_half == 0
        xpos, ypos = (jnp.where(turned, ypos, xpos), jnp.where(turned, xpos, ypos))
        level = level // 2
    order = jnp.argsort(curve, stable=True)
    order = jnp.take(order, (index + offset) % total)
    return (jnp.take(row, order), jnp.take(col, order))


def draw_tile_source_block(key, part):
    return curve_cells(key)[0].astype(jnp.int32)


def draw_tile_receiver_block(key, part):
    return curve_cells(key)[1].astype(jnp.int32)


def profile(key, length, rise):
    col_key, freq_key = jax.random.split(key)
    column = jnp.exp(jax.random.uniform(col_key, (length,), jnp.float32, -1.15, 1.15))
    ramp = jnp.exp(jnp.log(rise) * (jnp.arange(length, dtype=jnp.float32) / length - 0.5))
    per_freq = jnp.exp(jax.random.uniform(freq_key, (1, WINDOW_FREQS, 1, 1), jnp.float32, -0.35, 0.35))
    return per_freq * (column * ramp)[None, None, None, :]


def draw_data_vec(key, part):
    key = jax.random.fold_in(key, 31)
    base_key, scale_key = jax.random.split(key)
    base = jnp.clip(jax.random.normal(base_key, (2, WINDOW_FREQS, NVS, S), jnp.float32), -4.0, 4.0)
    rise = 3.0
    return base * profile(scale_key, S, rise)


def draw_direction(key, part):
    key = jax.random.fold_in(key, 47)
    base_key, scale_key = jax.random.split(key)
    base = jnp.clip(jax.random.normal(base_key, (2, WINDOW_FREQS, NVS, R), jnp.float32), -4.0, 4.0)
    rise = 3.0
    return base * profile(scale_key, R, rise)


def place_ends(array, key, low, high):
    index_at = [jax.random.randint(jax.random.fold_in(key, axis), (), 0, length) for axis, length in enumerate(array.shape)]
    longest = array.shape.index(max(array.shape))
    neighbour = index_at[:longest] + [(index_at[longest] + 1) % array.shape[longest]] + index_at[longest + 1:]
    return array.at[tuple(index_at)].set(low).at[tuple(neighbour)].set(high)


def level_of(stream_key, shape, pieces, low, high):
    loudness = 1.0
    for axis_at, parts in pieces:
        heights = jax.random.uniform(jax.random.fold_in(jax.random.fold_in(stream_key, 6), axis_at), (parts,), jnp.float32, low / len(pieces), high / len(pieces))
        loudness = loudness * jnp.repeat(jnp.exp(heights), shape[axis_at] // parts).reshape((-1,) + (1,) * (len(shape) - 1 - axis_at))
    return loudness


def scatter_about(key, shape, width, limit, cuts=(), held_as=jnp.bfloat16):
    loudness = level_of(key, shape, cuts, -0.22, 0.18) if cuts else 1.0
    array = jax.random.normal(key, shape, jnp.float32) * width * loudness
    return jnp.minimum(jnp.maximum(array, -limit), limit).astype(held_as)


def setup_inputs(seed: int = 0) -> dict:
    seeds = jax.random.split(jax.random.key(seed), 12)
    return {
        "data_vec": draw_data_vec(jax.random.fold_in(seeds[11], 71), 0),
        "direction": draw_direction(jax.random.fold_in(seeds[11], 71), 0),
        "model": scatter_about(seeds[2], (2, WINDOW_FREQS, NVS, R), 1.0, 6.0, ((1, 4), (3, 32)), jnp.float32),
        "alpha": jnp.clip(jax.random.uniform(seeds[3], (), jnp.float32, 0.5, 2.0), 0.5, 2.0),
        "u_factor": scatter_about(seeds[4], (WINDOW_FREQS, TILES, 2, RMAX, TILE_EXTENT), (RECEIVER_BLOCKS * 32) ** -0.5, 0.125, ((0, 4), (1, 32))),
        "v_factor": scatter_about(seeds[5], (WINDOW_FREQS, TILES, 2, RMAX, TILE_EXTENT), TILE_EXTENT ** -0.5, 0.375, ((0, 4), (1, 32))),
        "ranks": place_ends(jax.random.randint(seeds[6], (WINDOW_FREQS, TILES), RLO, RMAX + 1), jax.random.fold_in(seeds[6], 1), RLO, RMAX).astype(jnp.int32),
        "tile_source_block": draw_tile_source_block(jax.random.fold_in(seeds[11], 71), 0),
        "tile_receiver_block": draw_tile_receiver_block(jax.random.fold_in(seeds[11], 71), 0),
        "time_lo": place_ends(jax.random.randint(seeds[9], (R,), 0, NT // 2), jax.random.fold_in(seeds[9], 1), 0, (NT // 2) - 1).astype(jnp.int32),
        "time_len": place_ends(jax.random.randint(seeds[10], (R,), NT // 4, NT // 2 + 1), jax.random.fold_in(seeds[10], 1), NT // 4, (NT // 2 + 1) - 1).astype(jnp.int32),
    }


shrink_level = 0.5
eps = 1e-06

def tile_apply(first, second, keep, tile_pieces):
    hp = lax.Precision.HIGHEST
    fr = first[:, 0].astype(jnp.float32)
    fi = first[:, 1].astype(jnp.float32)
    sr = second[:, 0].astype(jnp.float32)
    si = second[:, 1].astype(jnp.float32)
    pr = tile_pieces[0].astype(jnp.float32)
    pim = tile_pieces[1].astype(jnp.float32)
    zr = jnp.einsum('trk,vtk->vtr', fr, pr, precision=hp) + jnp.einsum('trk,vtk->vtr', fi, pim, precision=hp)
    zi = jnp.einsum('trk,vtk->vtr', fr, pim, precision=hp) - jnp.einsum('trk,vtk->vtr', fi, pr, precision=hp)
    zr = lax.optimization_barrier((zr * keep).astype(jnp.bfloat16)).astype(jnp.float32)
    zi = lax.optimization_barrier((zi * keep).astype(jnp.bfloat16)).astype(jnp.float32)
    cr = jnp.einsum('trk,vtr->vtk', sr, zr, precision=hp) - jnp.einsum('trk,vtr->vtk', si, zi, precision=hp)
    ci = jnp.einsum('trk,vtr->vtk', sr, zi, precision=hp) + jnp.einsum('trk,vtr->vtk', si, zr, precision=hp)
    return (cr, ci)

def shrink(wide, lo, length, first, count):
    hp = lax.Precision.HIGHEST
    steps = jnp.arange(NT, dtype=jnp.int32)
    bins = FLO + jnp.arange(WINDOW_FREQS, dtype=jnp.int32)
    phase = (bins[:, None] * steps[None, :] % NT).astype(jnp.float32) * (2.0 * math.pi / NT)
    cosine = jnp.cos(phase)
    sine = jnp.sin(phase)
    signal = (jnp.einsum('kn,kvr->nvr', cosine, wide[0], precision=hp) - jnp.einsum('kn,kvr->nvr', sine, wide[1], precision=hp)) / math.sqrt(WINDOW_FREQS)
    moment = steps[:, None, None]
    inside = (moment >= lo[None, None, :]) & (moment < (lo + length)[None, None, :])
    kept = jnp.where(inside, jnp.sign(signal) * jnp.maximum(jnp.abs(signal) - shrink_level, 0.0), 0.0)
    own_cos = lax.dynamic_slice_in_dim(cosine, first, count, 0)
    own_sin = lax.dynamic_slice_in_dim(sine, first, count, 0)
    factor = 2.0 * math.sqrt(WINDOW_FREQS) / NT
    back_re = factor * jnp.einsum('kn,nvr->kvr', own_cos, kept, precision=hp)
    back_im = -factor * jnp.einsum('kn,nvr->kvr', own_sin, kept, precision=hp)
    return jnp.stack([back_re, back_im])

def reference(data_vec, direction, model, alpha, u_factor, v_factor, ranks, tile_source_block, tile_receiver_block, time_lo, time_len):
    count = RMAX
    model_blocks = jnp.moveaxis(direction.astype(jnp.bfloat16).reshape(2, WINDOW_FREQS, NVS, RECEIVER_BLOCKS, TILE_EXTENT), 1, 0)

    def forward_one(items):
        left, right, rank, block_list = items
        keep = (jnp.arange(count, dtype=jnp.int32)[None, :] < rank[:, None]).astype(jnp.float32)[None]
        tile_pieces = jnp.take(block_list, tile_receiver_block, axis=2)
        cr, ci = tile_apply(right, left, keep, tile_pieces)
        output_real = jnp.zeros((NVS, NRB, TILE_EXTENT), jnp.float32).at[:, tile_source_block].add(cr)
        output_imaginary = jnp.zeros((NVS, NRB, TILE_EXTENT), jnp.float32).at[:, tile_source_block].add(ci)
        return jnp.stack([output_real, output_imaginary]).reshape(2, NVS, S)
    forward = jnp.moveaxis(lax.map(forward_one, (u_factor, v_factor, ranks, model_blocks)), 0, 1)
    u_raw = forward - alpha * data_vec
    beta = jnp.sqrt(jnp.mean(u_raw * u_raw) + eps)
    u_next = u_raw / beta
    data_blocks = jnp.moveaxis(u_next.astype(jnp.bfloat16).reshape(2, WINDOW_FREQS, NVS, NRB, TILE_EXTENT), 1, 0)

    def adjoint_one(items):
        left, right, rank, block_list = items
        keep = (jnp.arange(count, dtype=jnp.int32)[None, :] < rank[:, None]).astype(jnp.float32)[None]
        tile_pieces = jnp.take(block_list, tile_source_block, axis=2)
        cr, ci = tile_apply(left, right, keep, tile_pieces)
        output_real = jnp.zeros((NVS, RECEIVER_BLOCKS, TILE_EXTENT), jnp.float32).at[:, tile_receiver_block].add(cr)
        output_imaginary = jnp.zeros((NVS, RECEIVER_BLOCKS, TILE_EXTENT), jnp.float32).at[:, tile_receiver_block].add(ci)
        return jnp.stack([output_real, output_imaginary]).reshape(2, NVS, R)
    adjoint = jnp.moveaxis(lax.map(adjoint_one, (u_factor, v_factor, ranks, data_blocks)), 0, 1)
    v_raw = adjoint - beta * direction
    alpha_next = jnp.sqrt(jnp.mean(v_raw * v_raw) + eps)
    v_next = v_raw / alpha_next
    wide = model + v_next
    model_next = shrink(wide, time_lo, time_len, 0, WINDOW_FREQS)
    return (u_next, v_next, model_next)
```

```python
import math

import jax
import jax.numpy as jnp
import ml_dtypes
import numpy as np
from jax import lax
from jax.experimental import pallas as pl
from jax.experimental.pallas import tpu as pltpu
from jax.sharding import PartitionSpec as P

WINDOW_FREQS = 64
NT = 512
FLO = 8
TILE_EXTENT = 256
RMAX = 48
RECEIVER_BLOCKS = 60
NVS = 4
SLOTS = 8

shrink_level = 0.5
eps = 1e-06

F32 = jnp.float32
BF16 = jnp.bfloat16
VMEM = pltpu.VMEM
SMEM = pltpu.SMEM
LIMIT = 50 * 1024 * 1024


def iota(shape, axis):
    return lax.broadcasted_iota(jnp.int32, shape, axis)


def low_rows():
    return iota((8, 128), 0) < 4


def swap(x):
    return pltpu.roll(x, 4, 0)


def call(body, outs, ins, scratch=(), out_spaces=None, **kw):
    out_spaces = out_spaces or [VMEM] * len(outs)
    return pl.pallas_call(
        body,
        out_shape=outs,
        in_specs=[pl.BlockSpec(memory_space=s) for s in ins],
        out_specs=[pl.BlockSpec(memory_space=s) for s in out_spaces],
        scratch_shapes=list(scratch),
        compiler_params=pltpu.CompilerParams(vmem_limit_bytes=LIMIT),
        **kw,
    )


def pack_body(rb, direction, data, out, slot_of, mark, ids):
    def clear(b, _):
        mark[b] = -1
        return 0

    lax.fori_loop(0, 64, clear, 0)
    for m in range(SLOTS):
        ids[m] = 0
    count = jnp.int32(0)
    for t in range(rb.shape[0]):
        b = rb[t]
        seen = mark[b]
        slot = jnp.minimum(jnp.where(seen < 0, count, seen), SLOTS - 1)
        mark[b] = slot
        ids[slot] = b
        slot_of[t] = slot
        count = count + jnp.where(seen < 0, 1, 0)
    lane = iota((4, 128), 1)
    listed = jnp.zeros((4, 128), F32)
    for m in range(SLOTS):
        listed = jnp.where(lane == 64 + m, ids[m].astype(F32), listed)
    for f in range(direction.shape[1]):
        for c in range(2):
            k = 2 * f + c
            out[k, :, 0:480] = direction[c, f]
            out[k, :, 512:640] = listed
            out[k, :, 512:576] = data[c, f]


def split_model_body(model, out):
    for f in range(model.shape[1]):
        both = jnp.concatenate([model[0, f], model[1, f]], axis=0)
        both = jnp.concatenate([both, jnp.zeros((8, 32), F32)], axis=1)
        for g in range(4):
            part = pltpu.roll(both, 512 - 120 * g, 1) if g else both
            part = part[:, 0:128]
            out[g, 2 * f] = part[0:4]
            out[g, 2 * f + 1] = part[4:8]


def blocks_of(chunks, half):
    low = low_rows()
    blocks = [None] * (2 * half)
    for b in range(half):
        even, odd = chunks[2 * b], chunks[2 * b + 1]
        blocks[b] = jnp.where(low, even, swap(odd))
        blocks[b + half] = jnp.where(low, swap(even), odd)
    return blocks


def spread_body(ids, rows, out, direction, data):
    lane = iota((8, 640), 1)
    chunks = [None] * 60
    tails = []
    for j in range(16):
        both = jnp.concatenate([rows[j], rows[j + 16]], axis=0)
        tails.append(both[:, 512:640])
        shift, first = 480 * j % 128, 480 * j // 128
        moved = jnp.where(lane < 480, both, 0.0)
        if shift:
            moved = pltpu.roll(moved, shift, 1)
        for q in range((shift + 479) // 128 + 1):
            piece = moved[:, 128 * q : 128 * q + 128]
            n = first + q
            chunks[n] = piece if chunks[n] is None else chunks[n] + piece
    for b, block in enumerate(blocks_of(chunks, 30)):
        direction[b] = block
    left = iota((8, 128), 1) < 64
    ends = [jnp.where(left, tails[2 * n], pltpu.roll(tails[2 * n + 1], 64, 1)) for n in range(8)]
    for b, block in enumerate(blocks_of(ends, 4)):
        data[b] = block

    def one(i, _):
        picked = [direction[ids[i, m]] for m in range(SLOTS)]
        out[i] = jnp.concatenate(picked, axis=0).astype(BF16)
        return 0

    lax.fori_loop(0, 32, one, 0, unroll=4)


def tiles_body(slot_in, slot_out, ranks, x, first, second, out, xs, acc):
    f = pl.program_id(0)
    low = low_rows()
    xr = x[0, 0:64].astype(F32)
    xi = x[1, 0:64].astype(F32)
    for m in range(SLOTS):
        tr = xr[8 * m : 8 * m + 8]
        ti = xi[8 * m : 8 * m + 8]
        tr4, ti4 = swap(tr), swap(ti)
        top = jnp.concatenate(
            [
                jnp.where(low, tr, ti4),
                jnp.where(low, tr4, ti),
                jnp.where(low, ti, -tr4),
                jnp.where(low, ti4, -tr),
            ],
            axis=1,
        )
        bottom = jnp.concatenate(
            [
                jnp.where(low, -ti, tr4),
                jnp.where(low, -ti4, tr),
                jnp.where(low, tr, ti4),
                jnp.where(low, tr4, ti),
            ],
            axis=1,
        )
        xs[m] = jnp.concatenate([top, bottom], axis=0).astype(BF16)
    acc[...] = jnp.zeros_like(acc)
    tiles = first.shape[1]
    lane = iota((16, RMAX), 1)
    for t in range(tiles):
        both = jnp.concatenate([first[0, t, 0], first[0, t, 1]], axis=1)
        z = lax.dot_general(
            xs[slot_in[t]], both, (((1,), (1,)), ((), ())), preferred_element_type=F32
        )
        z = jnp.where(lane < ranks[f, t], z, 0.0).astype(BF16)
        c = jnp.dot(z[0:8], second[0, t, 0], preferred_element_type=F32) + jnp.dot(
            z[8:16], second[0, t, 1], preferred_element_type=F32
        )
        at = slot_out[t]
        acc[at] = acc[at] + c
    for p in range(SLOTS // 2):
        real, imag = [], []
        for m in (2 * p, 2 * p + 1):
            left, right = acc[m, :, 0:128], acc[m, :, 128:256]
            real.append(jnp.where(low, left, swap(right)))
            imag.append(jnp.where(low, swap(left), right))
        out[0, 16 * p : 16 * p + 16] = jnp.concatenate(real, axis=0).astype(out.dtype)
        out[1, 16 * p : 16 * p + 16] = jnp.concatenate(imag, axis=0).astype(out.dtype)


def tile_products(slot_in, slot_out, ranks, x, first, second):
    freqs, tiles = first.shape[0], first.shape[1]
    factor = pl.BlockSpec((1, tiles, 2, RMAX, TILE_EXTENT), lambda f: (f, 0, 0, 0, 0))
    smem = pl.BlockSpec(memory_space=SMEM)
    return pl.pallas_call(
        tiles_body,
        grid=(freqs,),
        out_shape=jax.ShapeDtypeStruct((2 * freqs, 64, 128), BF16),
        in_specs=[
            smem,
            smem,
            smem,
            pl.BlockSpec((2, x.shape[1], 128), lambda f: (f, 0, 0)),
            factor,
            factor,
        ],
        out_specs=pl.BlockSpec((2, 64, 128), lambda f: (f, 0, 0)),
        scratch_shapes=[VMEM((SLOTS, 16, 512), BF16), VMEM((SLOTS, 8, 256), F32)],
        compiler_params=pltpu.CompilerParams(vmem_limit_bytes=LIMIT),
    )(slot_in, slot_out, ranks, x, first, second)


def residual_body(alpha, parts, data, out):
    total = parts[0].astype(F32)
    for i in range(1, 32):
        total = total + parts[i].astype(F32)
    u = total - alpha[0] * data[...].reshape(64, 128)
    square = u * u
    power = jnp.sum(jnp.sum(square, axis=0, keepdims=True), axis=1, keepdims=True)
    power = jnp.broadcast_to(power, (8, 128))
    s1 = power.astype(BF16).astype(F32)
    s2 = (power - s1).astype(BF16).astype(F32)
    s3 = power - s1 - s2
    row = iota((8, 128), 0)
    sums = jnp.where(row == 0, s1, jnp.where(row == 1, s2, jnp.where(row == 2, s3, 0.0)))
    ub = u.astype(BF16)
    high = ub.astype(F32)
    rest = u - high
    low = low_rows()
    for i in range(32):
        out[i, 0:64] = ub
    for b in range(8):
        hb, rb = high[8 * b : 8 * b + 8], rest[8 * b : 8 * b + 8]
        even = jnp.concatenate([jnp.where(low, hb, swap(rb)), sums], axis=0).astype(BF16)
        odd = jnp.concatenate([jnp.where(low, swap(hb), rb), sums], axis=0).astype(BF16)
        for n, tail in ((2 * b, even), (2 * b + 1, odd)):
            out[2 * n, 64:80] = tail
            out[2 * n + 1, 64:80] = tail


def update_body(ids, beta, parts, direction, out, acc):
    acc[...] = jnp.zeros_like(acc)

    def one(i, _):
        part = parts[i].astype(F32)
        for m in range(SLOTS):
            b = ids[i, m]
            acc[b] = acc[b] + part[8 * m : 8 * m + 8]
        return 0

    lax.fori_loop(0, 32, one, 0, unroll=2)
    low = low_rows()
    lane = iota((8, 128), 1)
    inverse, scale = beta[1], beta[0]
    chunks = [None] * 60
    power = jnp.zeros((8, 128), F32)
    for b in range(30):
        head = acc[b] * inverse - scale * direction[b]
        tail = acc[b + 30] * inverse - scale * direction[b + 30]
        power = power + head * head + tail * tail
        chunks[2 * b] = jnp.where(low, head, swap(tail))
        chunks[2 * b + 1] = jnp.where(low, swap(head), tail)
    power = jnp.sum(jnp.sum(power, axis=0, keepdims=True), axis=1, keepdims=True)
    power = jnp.broadcast_to(power, (8, 128))
    for d in range(64):
        n, off = 120 * d // 128, 120 * d % 128
        value = chunks[n]
        if off:
            value = pltpu.roll(value, 128 - off, 1)
        if off > 8:
            value = jnp.where(lane < 128 - off, value, pltpu.roll(chunks[n + 1], 128 - off, 1))
        value = jnp.where(lane == 120, power, value)
        j, g = d // 4, d % 4
        out[32 * g + j] = value[0:4]
        out[32 * g + j + 16] = value[4:8]


def split_dot(a_high, a_low, b):
    b_high = b.astype(BF16)
    b_low = (b - b_high.astype(F32)).astype(BF16)
    return (
        jnp.dot(a_high, b_high, preferred_element_type=F32)
        + jnp.dot(a_high, b_low, preferred_element_type=F32)
        + jnp.dot(a_low, b_high, preferred_element_type=F32)
    )


def shrink_body(raw, model, lo, hi, fh, fl, bh, bl, out):
    lane = iota((128, 128), 1)
    count = 2 * WINDOW_FREQS * NVS * RECEIVER_BLOCKS * TILE_EXTENT
    sums = jnp.where(lane == 120, raw[:, 0, :], 0.0)
    power = jnp.sum(jnp.sum(sums, axis=0, keepdims=True), axis=1, keepdims=True)
    alpha = jnp.sqrt(power / count + eps)
    moment = iota((NT, 128), 0)
    inside = (moment >= lo[...]) & (moment < hi[...])
    for v in range(NVS):
        step = raw[:, v, :] / alpha
        out[:, v, :] = step
        signal = split_dot(fh[...], fl[...], model[:, v, :] + step)
        kept = signal - jnp.clip(signal, -shrink_level, shrink_level)
        kept = jnp.where(inside, kept, 0.0)
        out[:, NVS + v, :] = split_dot(bh[...], bl[...], kept)


def finish_body(place, beta, back, tails, u_next, v_next, m_next):
    lane = iota((8, 128), 1)
    inverse = beta[1]
    odd = place[0] == 1
    for k in range(32):
        f, c = k // 2, k % 2
        quarter = [back[g, k] for g in range(4)]
        for q in range(4):
            value = quarter[q]
            if q:
                value = pltpu.roll(value, 128 - 8 * q, 1)
            if q < 3:
                value = jnp.where(
                    lane < 120 - 8 * q, value, pltpu.roll(quarter[q + 1], 120 - 8 * q, 1)
                )
            width = 128 if q < 3 else 96
            v_next[c, f, :, 128 * q : 128 * q + width] = value[0:4, 0:width]
            m_next[c, f, :, 128 * q : 128 * q + width] = value[4:8, 0:width]
        part = tails[k, 64:80].astype(F32)[0:8]
        part = (part + swap(part)) * inverse
        part = jnp.where(odd, pltpu.roll(part, 64, 1), part)
        u_next[c, f] = part[0:4, 0:64]


def transform_tables():
    steps = np.arange(NT)
    bins = FLO + np.arange(WINDOW_FREQS)
    phase = (bins[None, :] * steps[:, None] % NT) * (2.0 * math.pi / NT)
    table = np.stack([np.cos(phase), -np.sin(phase)], axis=2).reshape(NT, 2 * WINDOW_FREQS)
    forward = (table / math.sqrt(WINDOW_FREQS)).astype(np.float32)
    backward = (table.T * (2.0 * math.sqrt(WINDOW_FREQS) / NT)).astype(np.float32)
    out = []
    for a in (forward, backward):
        high = a.astype(ml_dtypes.bfloat16)
        out += [high, (a - high.astype(np.float32)).astype(ml_dtypes.bfloat16)]
    return out


def on_device(
    data_vec,
    direction,
    model,
    alpha,
    u_factor,
    v_factor,
    ranks,
    tile_source_block,
    tile_receiver_block,
    time_lo,
    time_len,
):
    shape = jax.ShapeDtypeStruct
    both = ("freq", "tile")
    g = lax.axis_index("freq")
    place = lax.axis_index("tile")

    def exchange(x, axis):
        return lax.all_to_all(x, axis, split_axis=0, concat_axis=0, tiled=True)

    packed, slots = call(
        pack_body,
        [shape((32, 4, 640), F32), shape((15,), jnp.int32)],
        [SMEM, VMEM, VMEM],
        [SMEM((64,), jnp.int32), SMEM((SLOTS,), jnp.int32)],
        [VMEM, SMEM],
    )(tile_receiver_block, direction, data_vec)
    rows = exchange(packed, "tile")

    (model_parts,) = call(split_model_body, [shape((4, 32, 4, 128), F32)], [VMEM])(model)
    model_all = exchange(model_parts, "freq").reshape(128, 4, 128)

    ids = rows[:, 0, 576 : 576 + SLOTS].astype(jnp.int32)
    picked, direction_rows, data_rows = call(
        spread_body,
        [shape((32, 64, 128), BF16), shape((60, 8, 128), F32), shape((8, 8, 128), F32)],
        [SMEM, VMEM],
    )(ids, rows)
    x = exchange(picked, "tile")
    parts = tile_products(slots, tile_source_block, ranks, x, v_factor, u_factor)
    parts = exchange(parts, "tile")
    (residual,) = call(residual_body, [shape((32, 80, 128), BF16)], [SMEM, VMEM, VMEM])(
        alpha.reshape(1), parts, data_rows
    )
    u_all = exchange(residual, "tile")

    left_count = 2 * WINDOW_FREQS * NVS * data_vec.shape[3] * 32
    power = jnp.sum(u_all[:, 72:75, 0].astype(F32))
    mine = jnp.broadcast_to(power, (8, 128))
    others = [
        lax.ppermute(mine, "freq", [(i, (i + d) % 4) for i in range(4)])[0, 0] for d in (1, 2, 3)
    ]
    total = (power + others[1]) + (others[0] + others[2])
    beta = jnp.sqrt(total / left_count + eps)
    beta = jnp.stack([beta, 1.0 / beta])

    back = tile_products(tile_source_block, slots, ranks, u_all, u_factor, v_factor)
    back = exchange(back, "tile")
    (raw,) = call(
        update_body,
        [shape((128, 4, 128), F32)],
        [SMEM, SMEM, VMEM, VMEM],
        [VMEM((64, 8, 128), F32)],
    )(ids, beta, back, direction_rows)
    raw = exchange(raw, both)

    lo = lax.dynamic_slice_in_dim(time_lo, g * 120, 120, 0)
    hi = lo + lax.dynamic_slice_in_dim(time_len, g * 120, 120, 0)
    lo = jnp.pad(lo, (0, 8)).reshape(1, 128)
    hi = jnp.pad(hi, (0, 8)).reshape(1, 128)
    tables = [jnp.asarray(a) for a in transform_tables()]
    (shrunk,) = call(shrink_body, [shape((128, 8, 128), F32)], [VMEM] * 8)(
        raw, model_all, lo, hi, *tables
    )
    shrunk = exchange(shrunk, "freq").reshape(4, 32, 8, 128)
    return call(
        finish_body,
        [
            shape(data_vec.shape, F32),
            shape(direction.shape, F32),
            shape(direction.shape, F32),
        ],
        [SMEM, SMEM, VMEM, VMEM],
    )((place % 2).reshape(1), beta, shrunk, u_all)


def solution(mesh):
    vector = P(None, "freq", None, "tile")
    factor = P("freq", "tile", None, None, None)
    placed = (
        vector,
        vector,
        vector,
        P(),
        factor,
        factor,
        P("freq", "tile"),
        P("tile"),
        P("tile"),
        P("tile"),
        P("tile"),
    )
    return jax.shard_map(
        on_device,
        mesh=mesh,
        in_specs=placed,
        out_specs=(vector, vector, vector),
        check_vma=False,
    )
```

```python
import functools
import math

import jax
import jax.numpy as jnp
import ml_dtypes
import numpy as np
from jax import lax
from jax.experimental import pallas as pl
from jax.experimental.pallas import tpu as pltpu
from jax.sharding import PartitionSpec as P

WINDOW_FREQS = 64
NT = 512
FLO = 8
TILE_EXTENT = 256
RMAX = 48
RECEIVER_BLOCKS = 60
NVS = 4
SLOTS = 8
GROUP = 4
LEFT_COUNT = 2 * WINDOW_FREQS * NVS * 2048

shrink_level = 0.5
eps = 1e-06

F32 = jnp.float32
BF16 = jnp.bfloat16
VMEM = pltpu.VMEM
SMEM = pltpu.SMEM
HBM = pltpu.HBM
LIMIT = 16 * 1024 * 1024
TILES_LIMIT = 50 * 1024 * 1024


def iota(shape, axis):
    return lax.broadcasted_iota(jnp.int32, shape, axis)


def low_rows():
    return iota((8, 128), 0) < 4


def swap(x):
    return pltpu.roll(x, 4, 0)


def call(body, outs, ins, scratch=(), out_spaces=None, limit=LIMIT):
    out_spaces = out_spaces or [VMEM] * len(outs)
    return pl.pallas_call(
        body,
        out_shape=outs,
        in_specs=[pl.BlockSpec(memory_space=s) for s in ins],
        out_specs=[pl.BlockSpec(memory_space=s) for s in out_spaces],
        scratch_shapes=list(scratch),
        compiler_params=pltpu.CompilerParams(vmem_limit_bytes=limit),
    )


def pack_body(rb, direction, data, model, out, slot_of, mark, ids, direction_in, data_in, model_in, sems):
    copies = [
        pltpu.make_async_copy(source, target, sems.at[n])
        for n, (source, target) in enumerate(
            ((direction, direction_in), (data, data_in), (model, model_in))
        )
    ]
    for copy in copies:
        copy.start()

    def clear(b, _):
        mark[b] = -1
        return 0

    lax.fori_loop(0, 64, clear, 0)
    for m in range(SLOTS):
        ids[m] = 0
    count = jnp.int32(0)
    for t in range(rb.shape[0]):
        b = rb[t]
        seen = mark[b]
        slot = jnp.minimum(jnp.where(seen < 0, count, seen), SLOTS - 1)
        mark[b] = slot
        ids[slot] = b
        slot_of[t] = slot
        count = count + jnp.where(seen < 0, 1, 0)
    lane = iota((4, 128), 1)
    listed = jnp.zeros((4, 128), F32)
    for m in range(SLOTS):
        listed = jnp.where(lane == 64 + m, ids[m].astype(F32), listed)
    for copy in copies:
        copy.wait()
    for f in range(direction.shape[1]):
        for c in range(2):
            k = 2 * f + c
            out[k, :, 0:480] = direction_in[c, f]
            out[k, :, 512:640] = listed
            out[k, :, 512:576] = data_in[c, f]
            out[k, :, 640:1120] = model_in[c, f]


def model_body(rows, out):
    lane = iota((8, 128), 1)
    for j in range(16):
        both = jnp.concatenate([rows[j, :, 640:1152], rows[j + 16, :, 640:1152]], axis=0)
        part = [both[:, 128 * q : 128 * q + 128] for q in range(4)]
        for g in range(4):
            value = part[0]
            if g:
                value = jnp.where(
                    lane < 8 * g,
                    pltpu.roll(part[g - 1], 8 * g, 1),
                    pltpu.roll(part[g], 8 * g, 1),
                )
            out[32 * g + j] = value[0:4]
            out[32 * g + j + 16] = value[4:8]


def blocks_of(chunks, half):
    low = low_rows()
    blocks = [None] * (2 * half)
    for b in range(half):
        even, odd = chunks[2 * b], chunks[2 * b + 1]
        blocks[b] = jnp.where(low, even, swap(odd))
        blocks[b + half] = jnp.where(low, swap(even), odd)
    return blocks


def spread_body(ids, rows, out, direction, data):
    lane = iota((8, 640), 1)
    chunks = [None] * 60
    tails = []
    for j in range(16):
        both = jnp.concatenate([rows[j, :, 0:640], rows[j + 16, :, 0:640]], axis=0)
        tails.append(both[:, 512:640])
        shift, first = 480 * j % 128, 480 * j // 128
        moved = jnp.where(lane < 480, both, 0.0)
        if shift:
            moved = pltpu.roll(moved, shift, 1)
        for q in range((shift + 479) // 128 + 1):
            piece = moved[:, 128 * q : 128 * q + 128]
            n = first + q
            chunks[n] = piece if chunks[n] is None else chunks[n] + piece
    for b, block in enumerate(blocks_of(chunks, 30)):
        direction[b] = block
    left = iota((8, 128), 1) < 64
    ends = [jnp.where(left, tails[2 * n], pltpu.roll(tails[2 * n + 1], 64, 1)) for n in range(8)]
    for b, block in enumerate(blocks_of(ends, 4)):
        data[b] = block

    def one(i, _):
        picked = [direction[ids[i, m]] for m in range(SLOTS)]
        out[i] = jnp.concatenate(picked, axis=0).astype(BF16)
        return 0

    lax.fori_loop(0, 32, one, 0, unroll=4)


def lanes_body(slots, blocks, ranks, lane_slot, lane_block, limit):
    tiles = ranks.shape[1]
    wide = RMAX * tiles
    lane = iota((8, wide), 1)
    for ref, out in ((slots, lane_slot), (blocks, lane_block)):
        value = jnp.full((8, wide), ref[0], jnp.int32)
        for t in range(1, tiles):
            value = jnp.where(lane >= RMAX * t, ref[t], value)
        out[...] = value
    tile, lane = iota((tiles, wide), 0), iota((tiles, wide), 1)
    within = lane - RMAX * tile
    spread = jnp.where((within >= 0) & (within < RMAX), 1.0, 0.0).astype(BF16)
    rank = jnp.dot(ranks[...].astype(F32).astype(BF16), spread, preferred_element_type=F32)
    start = jnp.zeros((1, wide), jnp.int32)
    lane = iota((1, wide), 1)
    for t in range(1, tiles):
        start = jnp.where(lane >= RMAX * t, RMAX * t, start)
    limit[...] = rank.astype(jnp.int32) + start


def tiles_body(extra, lane_in, lane_out, limits, x, first, second, *refs):
    rest, out = refs[:-1], refs[-1]
    tiles = first.shape[1]
    wide = RMAX * tiles
    low = low_rows()
    turned = (((1,), (1,)), ((), ()))
    source, target = lane_in[...], lane_out[...]
    lane = iota((8, wide), 1)
    upper = iota((8, wide), 0) < 4

    def one(f):
        xr = x[2 * f, 0:64].astype(F32)
        xi = x[2 * f + 1, 0:64].astype(F32)
        real, imag = [], []
        for m in range(SLOTS):
            tr = xr[8 * m : 8 * m + 8]
            ti = xi[8 * m : 8 * m + 8]
            tr4, ti4 = swap(tr), swap(ti)
            real.append(jnp.concatenate([jnp.where(low, tr, ti4), jnp.where(low, tr4, ti)], axis=1))
            imag.append(
                jnp.concatenate([jnp.where(low, ti, -tr4), jnp.where(low, ti4, -tr)], axis=1)
            )
        real = jnp.concatenate(real, axis=0).astype(BF16)
        imag = jnp.concatenate(imag, axis=0).astype(BF16)
        every = lax.dot_general(
            real, first[f, :, 0].reshape(wide, TILE_EXTENT), turned, preferred_element_type=F32
        ) + lax.dot_general(
            imag, first[f, :, 1].reshape(wide, TILE_EXTENT), turned, preferred_element_type=F32
        )
        z = every[0:8]
        for m in range(1, SLOTS):
            z = jnp.where(source == m, every[8 * m : 8 * m + 8], z)
        z = jnp.where(lane < limits[pl.ds(GROUP * pl.program_id(0) + f, 1)], z, 0.0)
        turn = pltpu.roll(z, 4, 0)
        turn = jnp.where(upper, -turn, turn)
        za = [jnp.where(target == m, z, 0.0) for m in range(SLOTS)]
        zb = [jnp.where(target == m, turn, 0.0) for m in range(SLOTS)]
        za = jnp.concatenate(za, axis=0).astype(BF16)
        zb = jnp.concatenate(zb, axis=0).astype(BF16)
        c = jnp.dot(
            za, second[f, :, 0].reshape(wide, TILE_EXTENT), preferred_element_type=F32
        ) + jnp.dot(zb, second[f, :, 1].reshape(wide, TILE_EXTENT), preferred_element_type=F32)
        real, imag = [], []
        for m in range(SLOTS):
            left, right = c[8 * m : 8 * m + 8, 0:128], c[8 * m : 8 * m + 8, 128:256]
            real.append(jnp.where(low, left, swap(right)))
            imag.append(jnp.where(low, swap(left), right))
        if extra:
            real[-1] = imag[-1] = rest[0][...]
        out[2 * f] = jnp.concatenate(real, axis=0).astype(out.dtype)
        out[2 * f + 1] = jnp.concatenate(imag, axis=0).astype(out.dtype)

    for f in range(GROUP):
        one(f)


def lane_tables(slots, blocks, ranks):
    wide = RMAX * ranks.shape[1]
    table = jax.ShapeDtypeStruct((8, wide), jnp.int32)
    limit = jax.ShapeDtypeStruct((ranks.shape[0], wide), jnp.int32)
    return call(lanes_body, [table, table, limit], [SMEM, SMEM, VMEM])(slots, blocks, ranks)


def tile_products(lane_in, lane_out, limits, x, first, second, *extra):
    freqs, tiles = first.shape[0], first.shape[1]
    whole = pl.BlockSpec(memory_space=VMEM)
    factor = pl.BlockSpec((GROUP, tiles, 2, RMAX, TILE_EXTENT), lambda f: (f, 0, 0, 0, 0))
    return pl.pallas_call(
        functools.partial(tiles_body, bool(extra)),
        grid=(freqs // GROUP,),
        out_shape=jax.ShapeDtypeStruct((2 * freqs, 64, 128), BF16),
        in_specs=[
            whole,
            whole,
            whole,
            pl.BlockSpec((2 * GROUP, x.shape[1], 128), lambda f: (f, 0, 0)),
            factor,
            factor,
        ]
        + [whole] * len(extra),
        out_specs=pl.BlockSpec((2 * GROUP, 64, 128), lambda f: (f, 0, 0)),
        compiler_params=pltpu.CompilerParams(vmem_limit_bytes=TILES_LIMIT),
    )(lane_in, lane_out, limits, x, first, second, *extra)


def residual_body(alpha, parts, data, out, power_out):
    total = parts[0].astype(F32)
    for i in range(1, 32):
        total = total + parts[i].astype(F32)
    u = total - alpha[0] * data[...].reshape(64, 128)
    power = jnp.sum(jnp.sum(u * u, axis=0, keepdims=True), axis=1, keepdims=True)
    power_out[...] = jnp.broadcast_to(power, (8, 128))
    ub = u.astype(BF16)
    high = ub.astype(F32)
    rest = u - high
    low = low_rows()
    empty = jnp.zeros((8, 128), F32)
    for i in range(32):
        out[i, 0:64] = ub
    for b in range(8):
        hb, rb = high[8 * b : 8 * b + 8], rest[8 * b : 8 * b + 8]
        even = jnp.concatenate([jnp.where(low, hb, swap(rb)), empty], axis=0).astype(BF16)
        odd = jnp.concatenate([jnp.where(low, swap(hb), rb), empty], axis=0).astype(BF16)
        for n, tail in ((2 * b, even), (2 * b + 1, odd)):
            out[2 * n, 64:80] = tail
            out[2 * n + 1, 64:80] = tail


def powers_body(own, p1, p2, p3, out):
    power = (own[...] + p2[...]) + (p1[...] + p3[...])
    s1 = power.astype(BF16).astype(F32)
    s2 = (power - s1).astype(BF16).astype(F32)
    s3 = power - s1 - s2
    row = iota((8, 128), 0)
    out[...] = jnp.where(row == 0, s1, jnp.where(row == 1, s2, jnp.where(row == 2, s3, 0.0)))


def update_body(ids, parts, direction, model, out, beta_out, acc):
    acc[...] = jnp.zeros_like(acc)

    def one(i, power):
        part = parts[i].astype(F32)
        for m in range(SLOTS - 1):
            b = ids[i, m]
            acc[b] = acc[b] + part[8 * m : 8 * m + 8]
        return power + part[56:64]

    power = lax.fori_loop(0, 32, one, jnp.zeros((8, 128), F32), unroll=2)
    power = jnp.broadcast_to(jnp.sum(power, axis=0, keepdims=True), (8, 128))
    scale = jnp.sqrt(power / LEFT_COUNT + eps)
    inverse = 1.0 / scale
    beta_out[...] = inverse
    low = low_rows()
    lane = iota((8, 128), 1)
    chunks = [None] * 60
    power = jnp.zeros((8, 128), F32)
    for b in range(30):
        head = acc[b] * inverse - scale * direction[b]
        tail = acc[b + 30] * inverse - scale * direction[b + 30]
        power = power + head * head + tail * tail
        chunks[2 * b] = jnp.where(low, head, swap(tail))
        chunks[2 * b + 1] = jnp.where(low, swap(head), tail)
    power = jnp.sum(jnp.sum(power, axis=0, keepdims=True), axis=1, keepdims=True)
    power = jnp.broadcast_to(power, (8, 128))
    for d in range(64):
        n, off = 120 * d // 128, 120 * d % 128
        value = chunks[n]
        if off:
            value = pltpu.roll(value, 128 - off, 1)
        if off > 8:
            value = jnp.where(lane < 128 - off, value, pltpu.roll(chunks[n + 1], 128 - off, 1))
        value = jnp.where(lane == 120, power, value)
        j, g = d // 4, d % 4
        for d, row in ((32 * g + j, value[0:4]), (32 * g + j + 16, value[4:8])):
            out[d, 0:4] = row
            out[d, 4:8] = model[d]


def split_dot(a_high, a_low, b):
    b_high = b.astype(BF16)
    b_low = (b - b_high.astype(F32)).astype(BF16)
    return (
        jnp.dot(a_high, b_high, preferred_element_type=F32)
        + jnp.dot(a_high, b_low, preferred_element_type=F32)
        + jnp.dot(a_low, b_high, preferred_element_type=F32)
    )


def shrink_body(raw, lo, hi, fh, fl, bh, bl, out):
    lane = iota((128, 128), 1)
    count = 2 * WINDOW_FREQS * NVS * RECEIVER_BLOCKS * TILE_EXTENT
    sums = jnp.where(lane == 120, raw[:, 0, :], 0.0)
    power = jnp.sum(jnp.sum(sums, axis=0, keepdims=True), axis=1, keepdims=True)
    alpha = jnp.sqrt(power / count + eps)
    moment = iota((NT, 128), 0)
    inside = (moment >= lo[...]) & (moment < hi[...])
    for v in range(NVS):
        step = raw[:, v, :] / alpha
        out[:, v, :] = step
        signal = split_dot(fh[...], fl[...], raw[:, NVS + v, :] + step)
        kept = signal - jnp.clip(signal, -shrink_level, shrink_level)
        kept = jnp.where(inside, kept, 0.0)
        out[:, NVS + v, :] = split_dot(bh[...], bl[...], kept)


def finish_body(place, beta, back, tails, u_next, v_next, m_next):
    lane = iota((8, 128), 1)
    inverse = beta[...]
    odd = place[0] == 1
    for k in range(32):
        f, c = k // 2, k % 2
        quarter = [back[g, k] for g in range(4)]
        for q in range(4):
            value = quarter[q]
            if q:
                value = pltpu.roll(value, 128 - 8 * q, 1)
            if q < 3:
                value = jnp.where(
                    lane < 120 - 8 * q, value, pltpu.roll(quarter[q + 1], 120 - 8 * q, 1)
                )
            width = 128 if q < 3 else 96
            v_next[c, f, :, 128 * q : 128 * q + width] = value[0:4, 0:width]
            m_next[c, f, :, 128 * q : 128 * q + width] = value[4:8, 0:width]
        part = tails[k, 64:80].astype(F32)[0:8]
        part = (part + swap(part)) * inverse
        part = jnp.where(odd, pltpu.roll(part, 64, 1), part)
        u_next[c, f] = part[0:4, 0:64]


def transform_tables():
    steps = np.arange(NT)
    bins = FLO + np.arange(WINDOW_FREQS)
    phase = (bins[None, :] * steps[:, None] % NT) * (2.0 * math.pi / NT)
    table = np.stack([np.cos(phase), -np.sin(phase)], axis=2).reshape(NT, 2 * WINDOW_FREQS)
    forward = (table / math.sqrt(WINDOW_FREQS)).astype(np.float32)
    backward = (table.T * (2.0 * math.sqrt(WINDOW_FREQS) / NT)).astype(np.float32)
    out = []
    for a in (forward, backward):
        high = a.astype(ml_dtypes.bfloat16)
        out += [high, (a - high.astype(np.float32)).astype(ml_dtypes.bfloat16)]
    return out


def on_device(
    data_vec,
    direction,
    model,
    alpha,
    u_factor,
    v_factor,
    ranks,
    tile_source_block,
    tile_receiver_block,
    time_lo,
    time_len,
):
    shape = jax.ShapeDtypeStruct
    both = ("freq", "tile")
    g = lax.axis_index("freq")
    place = lax.axis_index("tile")

    def exchange(x, axis):
        return lax.all_to_all(x, axis, split_axis=0, concat_axis=0, tiled=True)

    packed, slots = call(
        pack_body,
        [shape((32, 4, 1152), F32), shape((15,), jnp.int32)],
        [SMEM, HBM, HBM, HBM],
        [
            SMEM((64,), jnp.int32),
            SMEM((SLOTS,), jnp.int32),
            VMEM(direction.shape, F32),
            VMEM(data_vec.shape, F32),
            VMEM(model.shape, F32),
            pltpu.SemaphoreType.DMA((3,)),
        ],
        [VMEM, SMEM],
    )(tile_receiver_block, direction, data_vec, model)
    rows = exchange(packed, "tile")
    barrier = lax.optimization_barrier
    lanes = lane_tables(slots, tile_source_block, ranks)
    ids = rows[:, 0, 576 : 576 + SLOTS].astype(jnp.int32)
    ids, lanes = barrier((ids, lanes))
    lane_slot, lane_block, limits = lanes
    picked, direction_rows, data_rows = call(
        spread_body,
        [shape((32, 64, 128), BF16), shape((60, 8, 128), F32), shape((8, 8, 128), F32)],
        [SMEM, VMEM],
    )(ids, rows)
    x = exchange(picked, "tile")
    (model_rows,) = call(model_body, [shape((128, 4, 128), F32)], [VMEM])(rows)
    x, model_rows = barrier((x, model_rows))
    parts = tile_products(lane_slot, lane_block, limits, x, v_factor, u_factor)
    parts = exchange(parts, "tile")
    residual, power = call(
        residual_body,
        [shape((32, 80, 128), BF16), shape((8, 128), F32)],
        [SMEM, VMEM, VMEM],
    )(alpha.reshape(1), parts, data_rows)
    others = [lax.ppermute(power, "freq", [(i, (i + d) % 4) for i in range(4)]) for d in (1, 2, 3)]
    u_all = exchange(residual, "tile")
    (powers,) = call(powers_body, [shape((8, 128), F32)], [VMEM] * 4)(power, *others)

    back = tile_products(lane_block, lane_slot, limits, u_all, u_factor, v_factor, powers)
    back = exchange(back, "tile")
    raw, beta = call(
        update_body,
        [shape((128, 8, 128), F32), shape((8, 128), F32)],
        [SMEM, VMEM, VMEM, VMEM],
        [VMEM((64, 8, 128), F32)],
    )(ids, back, direction_rows, model_rows)
    raw = exchange(raw, both)

    lo = lax.dynamic_slice_in_dim(time_lo, g * 120, 120, 0)
    hi = lo + lax.dynamic_slice_in_dim(time_len, g * 120, 120, 0)
    lo = jnp.pad(lo, (0, 8)).reshape(1, 128)
    hi = jnp.pad(hi, (0, 8)).reshape(1, 128)
    tables = [jnp.asarray(a) for a in transform_tables()]
    (shrunk,) = call(shrink_body, [shape((128, 8, 128), F32)], [VMEM] * 7)(
        raw, lo, hi, *tables
    )
    shrunk = exchange(shrunk, "freq").reshape(4, 32, 8, 128)
    return call(
        finish_body,
        [
            shape(data_vec.shape, F32),
            shape(direction.shape, F32),
            shape(direction.shape, F32),
        ],
        [SMEM, VMEM, VMEM, VMEM],
    )((place % 2).reshape(1), beta, shrunk, u_all)


def solution(mesh):
    vector = P(None, "freq", None, "tile")
    factor = P("freq", "tile", None, None, None)
    placed = (
        vector,
        vector,
        vector,
        P(),
        factor,
        factor,
        P("freq", "tile"),
        P("tile"),
        P("tile"),
        P("tile"),
        P("tile"),
    )
    return jax.shard_map(
        on_device,
        mesh=mesh,
        in_specs=placed,
        out_specs=(vector, vector, vector),
        check_vma=False,
    )
```

```python
import functools
import math

import jax
import jax.numpy as jnp
import ml_dtypes
import numpy as np
from jax import lax
from jax.experimental import pallas as pl
from jax.experimental.pallas import tpu as pltpu
from jax.sharding import PartitionSpec as P

WINDOW_FREQS = 64
NT = 512
FLO = 8
TILE_EXTENT = 256
RMAX = 48
RECEIVER_BLOCKS = 60
NVS = 4
SLOTS = 8
GROUP = 4
LEFT_COUNT = 2 * WINDOW_FREQS * NVS * 2048

shrink_level = 0.5
eps = 1e-06

F32 = jnp.float32
BF16 = jnp.bfloat16
VMEM = pltpu.VMEM
SMEM = pltpu.SMEM
LIMIT = 16 * 1024 * 1024
TILES_LIMIT = 50 * 1024 * 1024


def iota(shape, axis):
    return lax.broadcasted_iota(jnp.int32, shape, axis)


def low_rows():
    return iota((8, 128), 0) < 4


def swap(x):
    return pltpu.roll(x, 4, 0)


def call(body, outs, ins, scratch=(), out_spaces=None, limit=LIMIT):
    out_spaces = out_spaces or [VMEM] * len(outs)
    return pl.pallas_call(
        body,
        out_shape=outs,
        in_specs=[pl.BlockSpec(memory_space=s) for s in ins],
        out_specs=[pl.BlockSpec(memory_space=s) for s in out_spaces],
        scratch_shapes=list(scratch),
        compiler_params=pltpu.CompilerParams(vmem_limit_bytes=limit),
    )


def pack_body(rb, direction, data, out, slot_of, mark, ids):
    def clear(b, _):
        mark[b] = -1
        return 0

    lax.fori_loop(0, 64, clear, 0)
    for m in range(SLOTS):
        ids[m] = 0
    count = jnp.int32(0)
    for t in range(rb.shape[0]):
        b = rb[t]
        seen = mark[b]
        slot = jnp.minimum(jnp.where(seen < 0, count, seen), SLOTS - 1)
        mark[b] = slot
        ids[slot] = b
        slot_of[t] = slot
        count = count + jnp.where(seen < 0, 1, 0)
    lane = iota((4, 128), 1)
    listed = jnp.zeros((4, 128), F32)
    for m in range(SLOTS):
        listed = jnp.where(lane == 64 + m, ids[m].astype(F32), listed)
    for f in range(direction.shape[1]):
        for c in range(2):
            k = 2 * f + c
            out[k, :, 0:480] = direction[c, f]
            out[k, :, 512:640] = listed
            out[k, :, 512:576] = data[c, f]


def model_body(group, model, out):
    lane = iota((8, 128), 1)
    for q in range(4):
        d = lax.rem(q + 4 - group[0], 4)
        for f in range(model.shape[1]):
            lo = max(q - 1, 0) * 128
            both = [model[c, f, :, lo : lo + (256 if 0 < q < 3 else 128 if q == 0 else 224)] for c in range(2)]
            both = jnp.concatenate(both, axis=0)
            if q == 0:
                value = both
            else:
                if q == 3:
                    both = jnp.concatenate([both, jnp.zeros((8, 32), F32)], axis=1)
                value = jnp.where(
                    lane < 8 * q,
                    pltpu.roll(both[:, 0:128], 8 * q, 1),
                    pltpu.roll(both[:, 128:256], 8 * q, 1),
                )
            out[d, 2 * f] = value[0:4]
            out[d, 2 * f + 1] = value[4:8]


def blocks_of(chunks, half):
    low = low_rows()
    blocks = [None] * (2 * half)
    for b in range(half):
        even, odd = chunks[2 * b], chunks[2 * b + 1]
        blocks[b] = jnp.where(low, even, swap(odd))
        blocks[b + half] = jnp.where(low, swap(even), odd)
    return blocks


def spread_body(ids, rows, out, direction, data):
    lane = iota((8, 640), 1)
    chunks = [None] * 60
    tails = []
    for j in range(16):
        both = jnp.concatenate([rows[j], rows[j + 16]], axis=0)
        tails.append(both[:, 512:640])
        shift, first = 480 * j % 128, 480 * j // 128
        moved = jnp.where(lane < 480, both, 0.0)
        if shift:
            moved = pltpu.roll(moved, shift, 1)
        for q in range((shift + 479) // 128 + 1):
            piece = moved[:, 128 * q : 128 * q + 128]
            n = first + q
            chunks[n] = piece if chunks[n] is None else chunks[n] + piece
    for b, block in enumerate(blocks_of(chunks, 30)):
        direction[b] = block
    left = iota((8, 128), 1) < 64
    ends = [jnp.where(left, tails[2 * n], pltpu.roll(tails[2 * n + 1], 64, 1)) for n in range(8)]
    for b, block in enumerate(blocks_of(ends, 4)):
        data[b] = block

    def one(i, _):
        picked = [direction[ids[i, m]] for m in range(SLOTS)]
        out[i] = jnp.concatenate(picked, axis=0).astype(BF16)
        return 0

    lax.fori_loop(0, 32, one, 0, unroll=4)


def lanes_body(slots, blocks, ranks, lane_slot, lane_block, limit):
    tiles = ranks.shape[1]
    wide = RMAX * tiles
    lane = iota((8, wide), 1)
    for ref, out in ((slots, lane_slot), (blocks, lane_block)):
        value = jnp.full((8, wide), ref[0], jnp.int32)
        for t in range(1, tiles):
            value = jnp.where(lane >= RMAX * t, ref[t], value)
        out[...] = value
    tile, lane = iota((tiles, wide), 0), iota((tiles, wide), 1)
    within = lane - RMAX * tile
    spread = jnp.where((within >= 0) & (within < RMAX), 1.0, 0.0).astype(BF16)
    rank = jnp.dot(ranks[...].astype(F32).astype(BF16), spread, preferred_element_type=F32)
    start = jnp.zeros((1, wide), jnp.int32)
    lane = iota((1, wide), 1)
    for t in range(1, tiles):
        start = jnp.where(lane >= RMAX * t, RMAX * t, start)
    limit[...] = rank.astype(jnp.int32) + start


def tiles_body(extra, lane_in, lane_out, limits, x, first, second, *refs):
    rest, out = refs[:-1], refs[-1]
    tiles = first.shape[1]
    wide = RMAX * tiles
    low = low_rows()
    turned = (((1,), (1,)), ((), ()))
    source, target = lane_in[...], lane_out[...]
    lane = iota((8, wide), 1)
    upper = iota((8, wide), 0) < 4

    def one(f):
        xr = x[2 * f, 0:64].astype(F32)
        xi = x[2 * f + 1, 0:64].astype(F32)
        real, imag = [], []
        for m in range(SLOTS):
            tr = xr[8 * m : 8 * m + 8]
            ti = xi[8 * m : 8 * m + 8]
            tr4, ti4 = swap(tr), swap(ti)
            real.append(jnp.concatenate([jnp.where(low, tr, ti4), jnp.where(low, tr4, ti)], axis=1))
            imag.append(
                jnp.concatenate([jnp.where(low, ti, -tr4), jnp.where(low, ti4, -tr)], axis=1)
            )
        real = jnp.concatenate(real, axis=0).astype(BF16)
        imag = jnp.concatenate(imag, axis=0).astype(BF16)
        every = lax.dot_general(
            real, first[f, :, 0].reshape(wide, TILE_EXTENT), turned, preferred_element_type=F32
        ) + lax.dot_general(
            imag, first[f, :, 1].reshape(wide, TILE_EXTENT), turned, preferred_element_type=F32
        )
        z = every[0:8]
        for m in range(1, SLOTS):
            z = jnp.where(source == m, every[8 * m : 8 * m + 8], z)
        z = jnp.where(lane < limits[pl.ds(GROUP * pl.program_id(0) + f, 1)], z, 0.0)
        turn = pltpu.roll(z, 4, 0)
        turn = jnp.where(upper, -turn, turn)
        za = [jnp.where(target == m, z, 0.0) for m in range(SLOTS)]
        zb = [jnp.where(target == m, turn, 0.0) for m in range(SLOTS)]
        za = jnp.concatenate(za, axis=0).astype(BF16)
        zb = jnp.concatenate(zb, axis=0).astype(BF16)
        c = jnp.dot(
            za, second[f, :, 0].reshape(wide, TILE_EXTENT), preferred_element_type=F32
        ) + jnp.dot(zb, second[f, :, 1].reshape(wide, TILE_EXTENT), preferred_element_type=F32)
        real, imag = [], []
        for m in range(SLOTS):
            left, right = c[8 * m : 8 * m + 8, 0:128], c[8 * m : 8 * m + 8, 128:256]
            real.append(jnp.where(low, left, swap(right)))
            imag.append(jnp.where(low, swap(left), right))
        if extra:
            real[-1] = imag[-1] = rest[0][...]
        out[2 * f] = jnp.concatenate(real, axis=0).astype(out.dtype)
        out[2 * f + 1] = jnp.concatenate(imag, axis=0).astype(out.dtype)

    for f in range(GROUP):
        one(f)


def lane_tables(slots, blocks, ranks):
    wide = RMAX * ranks.shape[1]
    table = jax.ShapeDtypeStruct((8, wide), jnp.int32)
    limit = jax.ShapeDtypeStruct((ranks.shape[0], wide), jnp.int32)
    return call(lanes_body, [table, table, limit], [SMEM, SMEM, VMEM])(slots, blocks, ranks)


def tile_products(lane_in, lane_out, limits, x, first, second, *extra):
    freqs, tiles = first.shape[0], first.shape[1]
    whole = pl.BlockSpec(memory_space=VMEM)
    factor = pl.BlockSpec((GROUP, tiles, 2, RMAX, TILE_EXTENT), lambda f: (f, 0, 0, 0, 0))
    return pl.pallas_call(
        functools.partial(tiles_body, bool(extra)),
        grid=(freqs // GROUP,),
        out_shape=jax.ShapeDtypeStruct((2 * freqs, 64, 128), BF16),
        in_specs=[
            whole,
            whole,
            whole,
            pl.BlockSpec((2 * GROUP, x.shape[1], 128), lambda f: (f, 0, 0)),
            factor,
            factor,
        ]
        + [whole] * len(extra),
        out_specs=pl.BlockSpec((2 * GROUP, 64, 128), lambda f: (f, 0, 0)),
        compiler_params=pltpu.CompilerParams(vmem_limit_bytes=TILES_LIMIT),
    )(lane_in, lane_out, limits, x, first, second, *extra)


def residual_body(alpha, parts, data, out, power_out):
    total = parts[0].astype(F32)
    for i in range(1, 32):
        total = total + parts[i].astype(F32)
    u = total - alpha[0] * data[...].reshape(64, 128)
    power = jnp.sum(jnp.sum(u * u, axis=0, keepdims=True), axis=1, keepdims=True)
    power_out[...] = jnp.broadcast_to(power, (8, 128))
    ub = u.astype(BF16)
    for i in range(32):
        out[i] = ub


def powers_body(own, p1, p2, p3, out):
    power = (own[...] + p2[...]) + (p1[...] + p3[...])
    s1 = power.astype(BF16).astype(F32)
    s2 = (power - s1).astype(BF16).astype(F32)
    s3 = power - s1 - s2
    row = iota((8, 128), 0)
    out[...] = jnp.where(row == 0, s1, jnp.where(row == 1, s2, jnp.where(row == 2, s3, 0.0)))


def update_body(ids, parts, direction, out, beta_out, acc):
    acc[...] = jnp.zeros_like(acc)

    def one(i, power):
        part = parts[i].astype(F32)
        for m in range(SLOTS - 1):
            b = ids[i, m]
            acc[b] = acc[b] + part[8 * m : 8 * m + 8]
        return power + part[56:64]

    power = lax.fori_loop(0, 32, one, jnp.zeros((8, 128), F32), unroll=2)
    power = jnp.broadcast_to(jnp.sum(power, axis=0, keepdims=True), (8, 128))
    scale = jnp.sqrt(power / LEFT_COUNT + eps)
    inverse = 1.0 / scale
    beta_out[...] = inverse
    low = low_rows()
    lane = iota((8, 128), 1)
    chunks = [None] * 60
    power = jnp.zeros((8, 128), F32)
    for b in range(30):
        head = acc[b] * inverse - scale * direction[b]
        tail = acc[b + 30] * inverse - scale * direction[b + 30]
        power = power + head * head + tail * tail
        chunks[2 * b] = jnp.where(low, head, swap(tail))
        chunks[2 * b + 1] = jnp.where(low, swap(head), tail)
    power = jnp.sum(jnp.sum(power, axis=0, keepdims=True), axis=1, keepdims=True)
    power = jnp.broadcast_to(power, (8, 128))
    for d in range(64):
        n, off = 120 * d // 128, 120 * d % 128
        value = chunks[n]
        if off:
            value = pltpu.roll(value, 128 - off, 1)
        if off > 8:
            value = jnp.where(lane < 128 - off, value, pltpu.roll(chunks[n + 1], 128 - off, 1))
        value = jnp.where(lane == 120, power, value)
        j, g = d // 4, d % 4
        out[32 * g + j] = value[0:4]
        out[32 * g + j + 16] = value[4:8]


def split_dot(a_high, a_low, b):
    b_high = b.astype(BF16)
    b_low = (b - b_high.astype(F32)).astype(BF16)
    return (
        jnp.dot(a_high, b_high, preferred_element_type=F32)
        + jnp.dot(a_high, b_low, preferred_element_type=F32)
        + jnp.dot(a_low, b_high, preferred_element_type=F32)
    )


def shrink_body(group, raw, m0, m1, m2, m3, lo, hi, fh, fl, bh, bl, out, model, both):
    for d, part in enumerate((m0, m1, m2, m3)):
        source = lax.rem(group[0] + 4 - d, 4)
        model[pl.ds(source * 32, 32)] = part[...]
    lane = iota((128, 128), 1)
    count = 2 * WINDOW_FREQS * NVS * RECEIVER_BLOCKS * TILE_EXTENT
    sums = jnp.where(lane == 120, raw[:, 0, :], 0.0)
    power = jnp.sum(jnp.sum(sums, axis=0, keepdims=True), axis=1, keepdims=True)
    alpha = jnp.sqrt(power / count + eps)
    moment = iota((NT, 128), 0)
    inside = (moment >= lo[...]) & (moment < hi[...])
    for v in range(NVS):
        step = raw[:, v, :] / alpha
        both[:, v, :] = step
        signal = split_dot(fh[...], fl[...], model[:, v, :] + step)
        kept = signal - jnp.clip(signal, -shrink_level, shrink_level)
        kept = jnp.where(inside, kept, 0.0)
        both[:, NVS + v, :] = split_dot(bh[...], bl[...], kept)
    out[...] = both[...].reshape(WINDOW_FREQS, 16, 128).astype(BF16)


def finish_body(place, beta, back, u, u_next, v_next, m_next):
    lane = iota((8, 128), 1)
    inverse = beta[...]
    block, half, odd = place[0] // 4, place[0] // 2 % 2 == 1, place[0] % 2 == 1
    for f in range(16):
        quarters = [back[g, f].astype(F32) for g in range(4)]
        for c in range(2):
            quarter = [x[8 * c : 8 * c + 8] for x in quarters]
            for q in range(4):
                value = quarter[q]
                if q:
                    value = pltpu.roll(value, 128 - 8 * q, 1)
                if q < 3:
                    value = jnp.where(
                        lane < 120 - 8 * q, value, pltpu.roll(quarter[q + 1], 120 - 8 * q, 1)
                    )
                width = 128 if q < 3 else 96
                v_next[c, f, :, 128 * q : 128 * q + width] = value[0:4, 0:width]
                m_next[c, f, :, 128 * q : 128 * q + width] = value[4:8, 0:width]
            every = u[2 * f + c].astype(F32)
            part = every[0:8]
            for b in range(1, 8):
                part = jnp.where(block == b, every[8 * b : 8 * b + 8], part)
            part = jnp.where(half, swap(part), part)
            part = jnp.where(odd, pltpu.roll(part, 64, 1), part)
            u_next[c, f] = (part * inverse)[0:4, 0:64]


def transform_tables():
    steps = np.arange(NT)
    bins = FLO + np.arange(WINDOW_FREQS)
    phase = (bins[None, :] * steps[:, None] % NT) * (2.0 * math.pi / NT)
    table = np.stack([np.cos(phase), -np.sin(phase)], axis=2).reshape(NT, 2 * WINDOW_FREQS)
    forward = (table / math.sqrt(WINDOW_FREQS)).astype(np.float32)
    backward = (table.T * (2.0 * math.sqrt(WINDOW_FREQS) / NT)).astype(np.float32)
    out = []
    for a in (forward, backward):
        high = a.astype(ml_dtypes.bfloat16)
        out += [high, (a - high.astype(np.float32)).astype(ml_dtypes.bfloat16)]
    return out


def on_device(
    data_vec,
    direction,
    model,
    alpha,
    u_factor,
    v_factor,
    ranks,
    tile_source_block,
    tile_receiver_block,
    time_lo,
    time_len,
):
    shape = jax.ShapeDtypeStruct
    both = ("freq", "tile")
    g = lax.axis_index("freq")
    place = lax.axis_index("tile")

    def exchange(x, axis):
        return lax.all_to_all(x, axis, split_axis=0, concat_axis=0, tiled=True)

    packed, slots = call(
        pack_body,
        [shape((32, 4, 640), F32), shape((15,), jnp.int32)],
        [SMEM, VMEM, VMEM],
        [SMEM((64,), jnp.int32), SMEM((SLOTS,), jnp.int32)],
        [VMEM, SMEM],
    )(tile_receiver_block, direction, data_vec)
    rows = exchange(packed, "tile")
    barrier = lax.optimization_barrier
    lanes = lane_tables(slots, tile_source_block, ranks)
    ids = rows[:, 0, 576 : 576 + SLOTS].astype(jnp.int32)
    ids, lanes = barrier((ids, lanes))
    lane_slot, lane_block, limits = lanes
    picked, direction_rows, data_rows = call(
        spread_body,
        [shape((32, 64, 128), BF16), shape((60, 8, 128), F32), shape((8, 8, 128), F32)],
        [SMEM, VMEM],
    )(ids, rows)
    x = exchange(picked, "tile")
    model, data_rows = barrier((model, data_rows))
    (model_parts,) = call(model_body, [shape((4, 32, 4, 128), F32)], [SMEM, VMEM])(g.reshape(1), model)
    models = [model_parts[0]] + [
        lax.ppermute(model_parts[d], "freq", [(i, (i + d) % 4) for i in range(4)]) for d in (1, 2, 3)
    ]
    x, models = barrier((x, models))
    parts = tile_products(lane_slot, lane_block, limits, x, v_factor, u_factor)
    parts = exchange(parts, "tile")
    residual, power = call(
        residual_body,
        [shape((32, 64, 128), BF16), shape((8, 128), F32)],
        [SMEM, VMEM, VMEM],
    )(alpha.reshape(1), parts, data_rows)
    others = [lax.ppermute(power, "freq", [(i, (i + d) % 4) for i in range(4)]) for d in (1, 2, 3)]
    u_all = exchange(residual, "tile")
    (powers,) = call(powers_body, [shape((8, 128), F32)], [VMEM] * 4)(power, *others)

    back = tile_products(lane_block, lane_slot, limits, u_all, u_factor, v_factor, powers)
    back = exchange(back, "tile")
    raw, beta = call(
        update_body,
        [shape((128, 4, 128), F32), shape((8, 128), F32)],
        [SMEM, VMEM, VMEM],
        [VMEM((64, 8, 128), F32)],
    )(ids, back, direction_rows)
    raw = exchange(raw, both)

    lo = lax.dynamic_slice_in_dim(time_lo, g * 120, 120, 0)
    hi = lo + lax.dynamic_slice_in_dim(time_len, g * 120, 120, 0)
    lo = jnp.pad(lo, (0, 8)).reshape(1, 128)
    hi = jnp.pad(hi, (0, 8)).reshape(1, 128)
    tables = [jnp.asarray(a) for a in transform_tables()]
    (shrunk,) = call(
        shrink_body,
        [shape((WINDOW_FREQS, 16, 128), BF16)],
        [SMEM] + [VMEM] * 11,
        [VMEM((128, 4, 128), F32), VMEM((128, 8, 128), F32)],
    )(g.reshape(1), raw, *models, lo, hi, *tables)
    shrunk = exchange(shrunk, "freq").reshape(4, 16, 16, 128)
    return call(
        finish_body,
        [
            shape(data_vec.shape, F32),
            shape(direction.shape, F32),
            shape(direction.shape, F32),
        ],
        [SMEM, VMEM, VMEM, VMEM],
    )(place.reshape(1), beta, shrunk, u_all)


def solution(mesh):
    vector = P(None, "freq", None, "tile")
    factor = P("freq", "tile", None, None, None)
    placed = (
        vector,
        vector,
        vector,
        P(),
        factor,
        factor,
        P("freq", "tile"),
        P("tile"),
        P("tile"),
        P("tile"),
        P("tile"),
    )
    return jax.shard_map(
        on_device,
        mesh=mesh,
        in_specs=placed,
        out_specs=(vector, vector, vector),
        check_vma=False,
    )
```

```python
import functools
import math

import jax
import jax.numpy as jnp
import ml_dtypes
import numpy as np
from jax import lax
from jax.experimental import pallas as pl
from jax.experimental.pallas import tpu as pltpu
from jax.sharding import PartitionSpec as P

WINDOW_FREQS = 64
NT = 512
FLO = 8
TILE_EXTENT = 256
RMAX = 48
RECEIVER_BLOCKS = 60
NVS = 4
SLOTS = 8
GROUP = 4
AHEAD = 2
LEFT_COUNT = 2 * WINDOW_FREQS * NVS * 2048

shrink_level = 0.5
eps = 1e-06

F32 = jnp.float32
BF16 = jnp.bfloat16
VMEM = pltpu.VMEM
SMEM = pltpu.SMEM
LIMIT = 16 * 1024 * 1024
TILES_LIMIT = 50 * 1024 * 1024


def iota(shape, axis):
    return lax.broadcasted_iota(jnp.int32, shape, axis)


def low_rows():
    return iota((8, 128), 0) < 4


def swap(x):
    return pltpu.roll(x, 4, 0)


def call(body, outs, ins, scratch=(), out_spaces=None, limit=LIMIT):
    out_spaces = out_spaces or [VMEM] * len(outs)
    return pl.pallas_call(
        body,
        out_shape=outs,
        in_specs=[pl.BlockSpec(memory_space=s) for s in ins],
        out_specs=[pl.BlockSpec(memory_space=s) for s in out_spaces],
        scratch_shapes=list(scratch),
        compiler_params=pltpu.CompilerParams(vmem_limit_bytes=limit),
    )


def pack_body(rb, direction, data, out, slot_of, mark, ids):
    def clear(b, _):
        mark[b] = -1
        return 0

    lax.fori_loop(0, 64, clear, 0)
    for m in range(SLOTS):
        ids[m] = 0
    count = jnp.int32(0)
    for t in range(rb.shape[0]):
        b = rb[t]
        seen = mark[b]
        slot = jnp.minimum(jnp.where(seen < 0, count, seen), SLOTS - 1)
        mark[b] = slot
        ids[slot] = b
        slot_of[t] = slot
        count = count + jnp.where(seen < 0, 1, 0)
    lane = iota((4, 128), 1)
    listed = jnp.zeros((4, 128), F32)
    for m in range(SLOTS):
        listed = jnp.where(lane == 64 + m, ids[m].astype(F32), listed)
    for f in range(direction.shape[1]):
        for c in range(2):
            k = 2 * f + c
            out[k, :, 0:480] = direction[c, f]
            out[k, :, 512:640] = listed
            out[k, :, 512:576] = data[c, f]


def model_body(model, out):
    for f in range(model.shape[1]):
        for c in range(2):
            rows = [model[c, f, :, 128 * q : 128 * q + 128] for q in range(3)]
            rows.append(jnp.concatenate([model[c, f, :, 384:480], jnp.zeros((4, 32), F32)], axis=1))
            out[2 * f + c] = jnp.concatenate(rows, axis=0).astype(BF16)


def blocks_of(chunks, half):
    low = low_rows()
    blocks = [None] * (2 * half)
    for b in range(half):
        even, odd = chunks[2 * b], chunks[2 * b + 1]
        blocks[b] = jnp.where(low, even, swap(odd))
        blocks[b + half] = jnp.where(low, swap(even), odd)
    return blocks


def spread_body(ids, rows, out, direction, data):
    lane = iota((8, 640), 1)
    chunks = [None] * 60
    tails = []
    for j in range(16):
        both = jnp.concatenate([rows[j], rows[j + 16]], axis=0)
        tails.append(both[:, 512:640])
        shift, first = 480 * j % 128, 480 * j // 128
        moved = jnp.where(lane < 480, both, 0.0)
        if shift:
            moved = pltpu.roll(moved, shift, 1)
        for q in range((shift + 479) // 128 + 1):
            piece = moved[:, 128 * q : 128 * q + 128]
            n = first + q
            chunks[n] = piece if chunks[n] is None else chunks[n] + piece
    for b, block in enumerate(blocks_of(chunks, 30)):
        direction[b] = block
    left = iota((8, 128), 1) < 64
    ends = [jnp.where(left, tails[2 * n], pltpu.roll(tails[2 * n + 1], 64, 1)) for n in range(8)]
    for b, block in enumerate(blocks_of(ends, 4)):
        data[b] = block

    def one(i, _):
        picked = [direction[ids[i, m]] for m in range(SLOTS)]
        out[i] = jnp.concatenate(picked, axis=0).astype(BF16)
        return 0

    lax.fori_loop(0, 32, one, 0, unroll=4)


def lanes_body(slots, blocks, ranks, lane_slot, lane_block, limit):
    tiles = ranks.shape[1]
    wide = RMAX * tiles
    lane = iota((8, wide), 1)
    for ref, out in ((slots, lane_slot), (blocks, lane_block)):
        value = jnp.full((8, wide), ref[0], jnp.int32)
        for t in range(1, tiles):
            value = jnp.where(lane >= RMAX * t, ref[t], value)
        out[...] = value
    tile, lane = iota((tiles, wide), 0), iota((tiles, wide), 1)
    within = lane - RMAX * tile
    spread = jnp.where((within >= 0) & (within < RMAX), 1.0, 0.0).astype(BF16)
    rank = jnp.dot(ranks[...].astype(F32).astype(BF16), spread, preferred_element_type=F32)
    start = jnp.zeros((1, wide), jnp.int32)
    lane = iota((1, wide), 1)
    for t in range(1, tiles):
        start = jnp.where(lane >= RMAX * t, RMAX * t, start)
    limit[...] = rank.astype(jnp.int32) + start


def tiles_body(extra, lane_in, lane_out, limits, x, first_hbm, second_hbm, *refs):
    rest, (out, first, second, sems) = refs[:-4], refs[-4:]
    steps = first.shape[0] // GROUP

    def copies(n):
        span = pl.ds(n * GROUP, GROUP)
        return [
            pltpu.make_async_copy(source.at[span], target.at[span], sems.at[a, n])
            for a, (source, target) in enumerate(((first_hbm, first), (second_hbm, second)))
        ]

    for n in range(AHEAD):
        for copy in copies(n):
            copy.start()
    tiles = first.shape[1]
    wide = RMAX * tiles
    low = low_rows()
    turned = (((1,), (1,)), ((), ()))
    source, target = lane_in[...], lane_out[...]
    lane = iota((8, wide), 1)
    upper = iota((8, wide), 0) < 4

    def one(f):
        xr = x[2 * f, 0:64].astype(F32)
        xi = x[2 * f + 1, 0:64].astype(F32)
        real, imag = [], []
        for m in range(SLOTS):
            tr = xr[8 * m : 8 * m + 8]
            ti = xi[8 * m : 8 * m + 8]
            tr4, ti4 = swap(tr), swap(ti)
            real.append(jnp.concatenate([jnp.where(low, tr, ti4), jnp.where(low, tr4, ti)], axis=1))
            imag.append(
                jnp.concatenate([jnp.where(low, ti, -tr4), jnp.where(low, ti4, -tr)], axis=1)
            )
        real = jnp.concatenate(real, axis=0).astype(BF16)
        imag = jnp.concatenate(imag, axis=0).astype(BF16)
        every = lax.dot_general(
            real, first[f, :, 0].reshape(wide, TILE_EXTENT), turned, preferred_element_type=F32
        ) + lax.dot_general(
            imag, first[f, :, 1].reshape(wide, TILE_EXTENT), turned, preferred_element_type=F32
        )
        z = every[0:8]
        for m in range(1, SLOTS):
            z = jnp.where(source == m, every[8 * m : 8 * m + 8], z)
        z = jnp.where(lane < limits[pl.ds(f, 1)], z, 0.0)
        turn = pltpu.roll(z, 4, 0)
        turn = jnp.where(upper, -turn, turn)
        za = [jnp.where(target == m, z, 0.0) for m in range(SLOTS)]
        zb = [jnp.where(target == m, turn, 0.0) for m in range(SLOTS)]
        za = jnp.concatenate(za, axis=0).astype(BF16)
        zb = jnp.concatenate(zb, axis=0).astype(BF16)
        c = jnp.dot(
            za, second[f, :, 0].reshape(wide, TILE_EXTENT), preferred_element_type=F32
        ) + jnp.dot(zb, second[f, :, 1].reshape(wide, TILE_EXTENT), preferred_element_type=F32)
        real, imag = [], []
        for m in range(SLOTS):
            left, right = c[8 * m : 8 * m + 8, 0:128], c[8 * m : 8 * m + 8, 128:256]
            real.append(jnp.where(low, left, swap(right)))
            imag.append(jnp.where(low, swap(left), right))
        if extra:
            real[-1] = imag[-1] = rest[0][...]
        out[2 * f] = jnp.concatenate(real, axis=0).astype(out.dtype)
        out[2 * f + 1] = jnp.concatenate(imag, axis=0).astype(out.dtype)

    def group(n, _):
        for copy in copies(n):
            copy.wait()

        @pl.when(n + AHEAD < steps)
        def _():
            for copy in copies(n + AHEAD):
                copy.start()

        for f in range(GROUP):
            one(n * GROUP + f)
        return 0

    lax.fori_loop(0, steps, group, 0)


def lane_tables(slots, blocks, ranks):
    wide = RMAX * ranks.shape[1]
    table = jax.ShapeDtypeStruct((8, wide), jnp.int32)
    limit = jax.ShapeDtypeStruct((ranks.shape[0], wide), jnp.int32)
    return call(lanes_body, [table, table, limit], [SMEM, SMEM, VMEM])(slots, blocks, ranks)


def tile_products(lane_in, lane_out, limits, x, first, second, *extra):
    return call(
        functools.partial(tiles_body, bool(extra)),
        [jax.ShapeDtypeStruct((2 * first.shape[0], 64, 128), BF16)],
        [VMEM] * 4 + [pltpu.HBM] * 2 + [VMEM] * len(extra),
        [
            VMEM(first.shape, BF16),
            VMEM(second.shape, BF16),
            pltpu.SemaphoreType.DMA((2, first.shape[0] // GROUP)),
        ],
        limit=TILES_LIMIT,
    )(lane_in, lane_out, limits, x, first, second, *extra)[0]


def residual_body(alpha, parts, data, out, power_out):
    total = parts[0].astype(F32)
    for i in range(1, 32):
        total = total + parts[i].astype(F32)
    u = total - alpha[0] * data[...].reshape(64, 128)
    power = jnp.sum(jnp.sum(u * u, axis=0, keepdims=True), axis=1, keepdims=True)
    power_out[...] = jnp.broadcast_to(power, (8, 128))
    ub = u.astype(BF16)
    for i in range(32):
        out[i] = ub


def powers_body(own, p1, p2, p3, out):
    power = (own[...] + p2[...]) + (p1[...] + p3[...])
    s1 = power.astype(BF16).astype(F32)
    s2 = (power - s1).astype(BF16).astype(F32)
    s3 = power - s1 - s2
    row = iota((8, 128), 0)
    out[...] = jnp.where(row == 0, s1, jnp.where(row == 1, s2, jnp.where(row == 2, s3, 0.0)))


def update_body(ids, parts, direction, out, beta_out, acc):
    acc[...] = jnp.zeros_like(acc)

    def one(i, power):
        part = parts[i].astype(F32)
        for m in range(SLOTS - 1):
            b = ids[i, m]
            acc[b] = acc[b] + part[8 * m : 8 * m + 8]
        return power + part[56:64]

    power = lax.fori_loop(0, 32, one, jnp.zeros((8, 128), F32), unroll=2)
    power = jnp.broadcast_to(jnp.sum(power, axis=0, keepdims=True), (8, 128))
    scale = jnp.sqrt(power / LEFT_COUNT + eps)
    inverse = 1.0 / scale
    beta_out[...] = inverse
    low = low_rows()
    lane = iota((8, 128), 1)
    chunks = [None] * 60
    power = jnp.zeros((8, 128), F32)
    for b in range(30):
        head = acc[b] * inverse - scale * direction[b]
        tail = acc[b + 30] * inverse - scale * direction[b + 30]
        power = power + head * head + tail * tail
        chunks[2 * b] = jnp.where(low, head, swap(tail))
        chunks[2 * b + 1] = jnp.where(low, swap(head), tail)
    power = jnp.sum(jnp.sum(power, axis=0, keepdims=True), axis=1, keepdims=True)
    power = jnp.broadcast_to(power, (8, 128))
    s1 = power.astype(BF16).astype(F32)
    s2 = (power - s1).astype(BF16).astype(F32)
    for j in range(16):
        rows = []
        for q in range(4):
            n, off = 480 * j // 128 + q, 480 * j % 128
            value = chunks[n]
            if off:
                value = pltpu.roll(value, 128 - off, 1)
                if n + 1 < 60:
                    after = pltpu.roll(chunks[n + 1], 128 - off, 1)
                    value = jnp.where(lane < 128 - off, value, after)
            rows.append(value)
        last = jnp.where(lane < 96, rows[3], 0.0)
        last = jnp.where(lane == 120, s1, jnp.where(lane == 121, s2, last))
        rows[3] = jnp.where(lane == 122, power - s1 - s2, last)
        first = [jnp.where(low, rows[q], swap(rows[q + 1])) for q in (0, 2)]
        second = [jnp.where(low, swap(rows[q]), rows[q + 1]) for q in (0, 2)]
        for d, value in ((j, first), (j + 16, second)):
            value = jnp.concatenate(value, axis=0).astype(BF16)
            for g in range(4):
                out[32 * g + d] = value


def halves(x):
    high = x.astype(BF16)
    return high, (x - high.astype(F32)).astype(BF16)


def shrink_body(group, raw, m0, m1, m2, m3, lo, hi, fh, fl, bh, bl, v_next, m_next, wide, back):
    g = group[0]
    for d, part in enumerate((m0, m1, m2, m3)):
        source = lax.rem(g + 4 - d, 4)
        wide[pl.ds(source * 32, 32)] = part[...].astype(F32)
    lane = iota((128, 128), 1)
    count = 2 * WINDOW_FREQS * NVS * RECEIVER_BLOCKS * TILE_EXTENT
    sums = raw[:, 0:16, :].astype(F32)[:, 12, :]
    sums = jnp.where((lane >= 120) & (lane < 123), sums, 0.0)
    power = jnp.sum(jnp.sum(sums, axis=0, keepdims=True), axis=1, keepdims=True)
    inverse = 1.0 / jnp.sqrt(power / count + eps)
    own = raw[pl.ds(g * 32, 32)].astype(F32) * inverse[None]
    for k in range(32):
        for q in range(4):
            width = 128 if q < 3 else 96
            at = slice(128 * q, 128 * q + width)
            v_next[k % 2, k // 2, :, at] = own[k, 4 * q : 4 * q + 4, 0:width]
    wide[...] = wide[...] + raw[...].astype(F32) * inverse[None]
    moment = iota((NT, 128), 0)
    table = jnp.concatenate([fh[...], fl[...]], axis=1)
    at = pl.ds(pl.multiple_of(g * 32, 32), 32)
    own_high, own_low = bh[at], bl[at]
    own_both = jnp.concatenate([own_high, own_low], axis=0)
    for q in range(4):
        inside = (moment >= lo[q : q + 1]) & (moment < hi[q : q + 1])
        inside = jnp.concatenate([inside, inside], axis=1)
        for v in range(0, NVS, 2):
            r = 4 * q + v
            high, low = halves(jnp.concatenate([wide[:, r, :], wide[:, r + 1, :]], axis=1))
            signal = jnp.dot(
                table, jnp.concatenate([high, high], axis=0), preferred_element_type=F32
            ) + jnp.dot(fh[...], low, preferred_element_type=F32)
            kept = signal - jnp.clip(signal, -shrink_level, shrink_level)
            high, low = halves(jnp.where(inside, kept, 0.0))
            result = jnp.dot(own_both, high, preferred_element_type=F32)
            result = result[0:32] + result[32:64]
            result = result + jnp.dot(own_high, low, preferred_element_type=F32)
            back[:, r, :] = result[:, 0:128]
            back[:, r + 1, :] = result[:, 128:256]
    for k in range(32):
        for q in range(4):
            width = 128 if q < 3 else 96
            at = slice(128 * q, 128 * q + width)
            m_next[k % 2, k // 2, :, at] = back[k, 4 * q : 4 * q + 4, 0:width]


def data_body(place, beta, u, u_next):
    inverse = beta[...]
    block, half, odd = place[0] // 4, place[0] // 2 % 2 == 1, place[0] % 2 == 1
    for k in range(32):
        every = u[k].astype(F32)
        part = every[0:8]
        for b in range(1, 8):
            part = jnp.where(block == b, every[8 * b : 8 * b + 8], part)
        part = jnp.where(half, swap(part), part)
        part = jnp.where(odd, pltpu.roll(part, 64, 1), part)
        u_next[k % 2, k // 2] = (part * inverse)[0:4, 0:64]


def transform_tables():
    steps = np.arange(NT)
    bins = FLO + np.arange(WINDOW_FREQS)
    phase = (bins[None, :] * steps[:, None] % NT) * (2.0 * math.pi / NT)
    table = np.stack([np.cos(phase), -np.sin(phase)], axis=2).reshape(NT, 2 * WINDOW_FREQS)
    forward = (table / math.sqrt(WINDOW_FREQS)).astype(np.float32)
    backward = (table.T * (2.0 * math.sqrt(WINDOW_FREQS) / NT)).astype(np.float32)
    out = []
    for a in (forward, backward):
        high = a.astype(ml_dtypes.bfloat16)
        out += [high, (a - high.astype(np.float32)).astype(ml_dtypes.bfloat16)]
    return out


def on_device(
    data_vec,
    direction,
    model,
    alpha,
    u_factor,
    v_factor,
    ranks,
    tile_source_block,
    tile_receiver_block,
    time_lo,
    time_len,
):
    shape = jax.ShapeDtypeStruct
    both = ("freq", "tile")
    g = lax.axis_index("freq")
    place = lax.axis_index("tile")

    def exchange(x, axis):
        return lax.all_to_all(x, axis, split_axis=0, concat_axis=0, tiled=True)

    packed, slots = call(
        pack_body,
        [shape((32, 4, 640), F32), shape((15,), jnp.int32)],
        [SMEM, VMEM, VMEM],
        [SMEM((64,), jnp.int32), SMEM((SLOTS,), jnp.int32)],
        [VMEM, SMEM],
    )(tile_receiver_block, direction, data_vec)
    rows = exchange(packed, "tile")
    barrier = lax.optimization_barrier
    lanes = lane_tables(slots, tile_source_block, ranks)
    ids = rows[:, 0, 576 : 576 + SLOTS].astype(jnp.int32)
    ids, lanes = barrier((ids, lanes))
    lane_slot, lane_block, limits = lanes
    picked, direction_rows, data_rows = call(
        spread_body,
        [shape((32, 64, 128), BF16), shape((60, 8, 128), F32), shape((8, 8, 128), F32)],
        [SMEM, VMEM],
    )(ids, rows)
    x = exchange(picked, "tile")
    model, data_rows = barrier((model, data_rows))
    (own_model,) = call(model_body, [shape((32, 16, 128), BF16)], [VMEM])(model)
    models = [own_model] + [
        lax.ppermute(own_model, "freq", [(i, (i + d) % 4) for i in range(4)]) for d in (1, 2, 3)
    ]
    parts = tile_products(lane_slot, lane_block, limits, x, v_factor, u_factor)
    parts, models = barrier((parts, models))
    parts = exchange(parts, "tile")
    residual, power = call(
        residual_body,
        [shape((32, 64, 128), BF16), shape((8, 128), F32)],
        [SMEM, VMEM, VMEM],
    )(alpha.reshape(1), parts, data_rows)
    others = [lax.ppermute(power, "freq", [(i, (i + d) % 4) for i in range(4)]) for d in (1, 2, 3)]
    u_all = exchange(residual, "tile")
    (powers,) = call(powers_body, [shape((8, 128), F32)], [VMEM] * 4)(power, *others)

    back = tile_products(lane_block, lane_slot, limits, u_all, u_factor, v_factor, powers)
    back = exchange(back, "tile")
    raw, beta = call(
        update_body,
        [shape((128, 16, 128), BF16), shape((8, 128), F32)],
        [SMEM, VMEM, VMEM],
        [VMEM((64, 8, 128), F32)],
    )(ids, back, direction_rows)
    raw = exchange(raw, both)

    (u_next,) = call(data_body, [shape(data_vec.shape, F32)], [SMEM, VMEM, VMEM])(
        place.reshape(1), beta, u_all
    )
    lo = jnp.pad(time_lo, (0, 32)).reshape(4, 128)
    hi = jnp.pad(time_lo + time_len, (0, 32)).reshape(4, 128)
    tables = [jnp.asarray(a) for a in transform_tables()]
    v_next, m_next = call(
        shrink_body,
        [shape(direction.shape, F32), shape(direction.shape, F32)],
        [SMEM] + [VMEM] * 11,
        [VMEM((128, 16, 128), F32), VMEM((32, 16, 128), F32)],
    )(g.reshape(1), raw, *models, lo, hi, *tables)
    return u_next, v_next, m_next


def solution(mesh):
    vector = P(None, "freq", None, "tile")
    factor = P("freq", "tile", None, None, None)
    placed = (
        vector,
        vector,
        vector,
        P(),
        factor,
        factor,
        P("freq", "tile"),
        P("tile"),
        P("tile"),
        P("tile"),
        P("tile"),
    )
    return jax.shard_map(
        on_device,
        mesh=mesh,
        in_specs=placed,
        out_specs=(vector, vector, vector),
        check_vma=False,
    )
```

```python
import functools
import math

import jax
import jax.numpy as jnp
import ml_dtypes
import numpy as np
from jax import lax
from jax.experimental import pallas as pl
from jax.experimental.pallas import tpu as pltpu
from jax.sharding import PartitionSpec as P

WINDOW_FREQS = 64
NT = 512
FLO = 8
TILE_EXTENT = 256
RMAX = 48
RECEIVER_BLOCKS = 60
NVS = 4
SLOTS = 8
GROUP = 4
AHEAD = 2
LEFT_COUNT = 2 * WINDOW_FREQS * NVS * 2048

shrink_level = 0.5
eps = 1e-06

F32 = jnp.float32
BF16 = jnp.bfloat16
VMEM = pltpu.VMEM
SMEM = pltpu.SMEM
LIMIT = 16 * 1024 * 1024
TILES_LIMIT = 50 * 1024 * 1024


def iota(shape, axis):
    return lax.broadcasted_iota(jnp.int32, shape, axis)


def low_rows():
    return iota((8, 128), 0) < 4


def swap(x):
    return pltpu.roll(x, 4, 0)


def call(body, outs, ins, scratch=(), out_spaces=None, limit=LIMIT):
    out_spaces = out_spaces or [VMEM] * len(outs)
    return pl.pallas_call(
        body,
        out_shape=outs,
        in_specs=[pl.BlockSpec(memory_space=s) for s in ins],
        out_specs=[pl.BlockSpec(memory_space=s) for s in out_spaces],
        scratch_shapes=list(scratch),
        compiler_params=pltpu.CompilerParams(vmem_limit_bytes=limit),
    )


def pack_body(rb, direction, out, slot_of, mark, ids):
    def clear(b, _):
        mark[b] = -1
        return 0

    lax.fori_loop(0, 64, clear, 0)
    for m in range(SLOTS):
        ids[m] = 0
    count = jnp.int32(0)
    for t in range(rb.shape[0]):
        b = rb[t]
        seen = mark[b]
        slot = jnp.minimum(jnp.where(seen < 0, count, seen), SLOTS - 1)
        mark[b] = slot
        ids[slot] = b
        slot_of[t] = slot
        count = count + jnp.where(seen < 0, 1, 0)
    lane = iota((4, 128), 1)
    listed = jnp.zeros((4, 128), F32)
    for m in range(SLOTS):
        listed = jnp.where(lane == 96 + m, ids[m].astype(F32), listed)
    for f in range(direction.shape[1]):
        for c in range(2):
            k = 2 * f + c
            out[k, :, 384:512] = listed
            out[k, :, 0:480] = direction[c, f]


def model_body(model, out):
    for f in range(model.shape[1]):
        for c in range(2):
            rows = [model[c, f, :, 128 * q : 128 * q + 128] for q in range(3)]
            rows.append(jnp.concatenate([model[c, f, :, 384:480], jnp.zeros((4, 32), F32)], axis=1))
            out[2 * f + c] = jnp.concatenate(rows, axis=0).astype(BF16)


def blocks_of(chunks, half):
    low = low_rows()
    blocks = [None] * (2 * half)
    for b in range(half):
        even, odd = chunks[2 * b], chunks[2 * b + 1]
        blocks[b] = jnp.where(low, even, swap(odd))
        blocks[b + half] = jnp.where(low, swap(even), odd)
    return blocks


def spread_body(ids, rows, data, out, direction):
    lane = iota((8, 512), 1)
    chunks = [None] * 60
    empty = jnp.zeros((8, 128), F32)
    for j in range(16):
        both = jnp.concatenate([rows[j], rows[j + 16]], axis=0)
        shift, first = 480 * j % 128, 480 * j // 128
        moved = jnp.concatenate([jnp.where(lane < 480, both, 0.0), empty], axis=1)
        if shift:
            moved = pltpu.roll(moved, shift, 1)
        for q in range((shift + 479) // 128 + 1):
            piece = moved[:, 128 * q : 128 * q + 128]
            n = first + q
            chunks[n] = piece if chunks[n] is None else chunks[n] + piece
    for b, block in enumerate(blocks_of(chunks, 30)):
        direction[b] = block

    def one(i, _):
        picked = [direction[ids[i, m]] for m in range(SLOTS - 1)]
        picked.append(data[i])
        out[i] = jnp.concatenate(picked, axis=0).astype(BF16)
        return 0

    lax.fori_loop(0, 32, one, 0, unroll=4)


def lanes_body(slots, blocks, ranks, data, lane_slot, lane_block, limit, data_rows):
    tiles = ranks.shape[1]
    wide = RMAX * tiles
    lane = iota((8, wide), 1)
    for ref, out in ((slots, lane_slot), (blocks, lane_block)):
        value = jnp.full((8, wide), ref[0], jnp.int32)
        for t in range(1, tiles):
            value = jnp.where(lane >= RMAX * t, ref[t], value)
        out[...] = value
    tile, lane = iota((tiles, wide), 0), iota((tiles, wide), 1)
    within = lane - RMAX * tile
    spread = jnp.where((within >= 0) & (within < RMAX), 1.0, 0.0).astype(BF16)
    rank = jnp.dot(ranks[...].astype(F32).astype(BF16), spread, preferred_element_type=F32)
    start = jnp.zeros((1, wide), jnp.int32)
    lane = iota((1, wide), 1)
    for t in range(1, tiles):
        start = jnp.where(lane >= RMAX * t, RMAX * t, start)
    limit[...] = rank.astype(jnp.int32) + start
    for k in range(32):
        own = data[k % 2, k // 2]
        high = own.astype(BF16).astype(F32)
        own = jnp.concatenate([high, own - high], axis=1)
        data_rows[k] = jnp.concatenate([own, jnp.zeros((4, 128), F32)], axis=0)


def tiles_body(extra, lane_in, lane_out, limits, x, first_hbm, second_hbm, *refs):
    rest, (out, first, second, sems) = refs[:-4], refs[-4:]
    steps = first.shape[0] // GROUP

    def copies(n):
        span = pl.ds(n * GROUP, GROUP)
        return [
            pltpu.make_async_copy(source.at[span], target.at[span], sems.at[a, n])
            for a, (source, target) in enumerate(((first_hbm, first), (second_hbm, second)))
        ]

    for n in range(AHEAD):
        for copy in copies(n):
            copy.start()
    tiles = first.shape[1]
    wide = RMAX * tiles
    low = low_rows()
    turned = (((1,), (1,)), ((), ()))
    source, target = lane_in[...], lane_out[...]
    lane = iota((8, wide), 1)
    upper = iota((8, wide), 0) < 4

    def one(f):
        xr = x[2 * f, 0:64].astype(F32)
        xi = x[2 * f + 1, 0:64].astype(F32)
        real, imag = [], []
        for m in range(SLOTS):
            tr = xr[8 * m : 8 * m + 8]
            ti = xi[8 * m : 8 * m + 8]
            tr4, ti4 = swap(tr), swap(ti)
            real.append(jnp.concatenate([jnp.where(low, tr, ti4), jnp.where(low, tr4, ti)], axis=1))
            imag.append(
                jnp.concatenate([jnp.where(low, ti, -tr4), jnp.where(low, ti4, -tr)], axis=1)
            )
        real = jnp.concatenate(real, axis=0).astype(BF16)
        imag = jnp.concatenate(imag, axis=0).astype(BF16)
        every = lax.dot_general(
            real, first[f, :, 0].reshape(wide, TILE_EXTENT), turned, preferred_element_type=F32
        ) + lax.dot_general(
            imag, first[f, :, 1].reshape(wide, TILE_EXTENT), turned, preferred_element_type=F32
        )
        z = every[0:8]
        for m in range(1, SLOTS):
            z = jnp.where(source == m, every[8 * m : 8 * m + 8], z)
        z = jnp.where(lane < limits[pl.ds(f, 1)], z, 0.0)
        turn = pltpu.roll(z, 4, 0)
        turn = jnp.where(upper, -turn, turn)
        za = [jnp.where(target == m, z, 0.0) for m in range(SLOTS)]
        zb = [jnp.where(target == m, turn, 0.0) for m in range(SLOTS)]
        za = jnp.concatenate(za, axis=0).astype(BF16)
        zb = jnp.concatenate(zb, axis=0).astype(BF16)
        c = jnp.dot(
            za, second[f, :, 0].reshape(wide, TILE_EXTENT), preferred_element_type=F32
        ) + jnp.dot(zb, second[f, :, 1].reshape(wide, TILE_EXTENT), preferred_element_type=F32)
        real, imag = [], []
        for m in range(SLOTS):
            left, right = c[8 * m : 8 * m + 8, 0:128], c[8 * m : 8 * m + 8, 128:256]
            real.append(jnp.where(low, left, swap(right)))
            imag.append(jnp.where(low, swap(left), right))
        if extra:
            real[-1] = imag[-1] = rest[0][...]
        out[2 * f] = jnp.concatenate(real, axis=0).astype(out.dtype)
        out[2 * f + 1] = jnp.concatenate(imag, axis=0).astype(out.dtype)

    def group(n, _):
        for copy in copies(n):
            copy.wait()

        @pl.when(n + AHEAD < steps)
        def _():
            for copy in copies(n + AHEAD):
                copy.start()

        for f in range(GROUP):
            one(n * GROUP + f)
        return 0

    lax.fori_loop(0, steps, group, 0)


def lane_tables(slots, blocks, ranks, data):
    wide = RMAX * ranks.shape[1]
    table = jax.ShapeDtypeStruct((8, wide), jnp.int32)
    limit = jax.ShapeDtypeStruct((ranks.shape[0], wide), jnp.int32)
    rows = jax.ShapeDtypeStruct((32, 8, 128), F32)
    return call(lanes_body, [table, table, limit, rows], [SMEM, SMEM, VMEM, VMEM])(
        slots, blocks, ranks, data
    )


def tile_products(lane_in, lane_out, limits, x, first, second, *extra):
    return call(
        functools.partial(tiles_body, bool(extra)),
        [jax.ShapeDtypeStruct((2 * first.shape[0], 64, 128), BF16)],
        [VMEM] * 4 + [pltpu.HBM] * 2 + [VMEM] * len(extra),
        [
            VMEM(first.shape, BF16),
            VMEM(second.shape, BF16),
            pltpu.SemaphoreType.DMA((2, first.shape[0] // GROUP)),
        ],
        limit=TILES_LIMIT,
    )(lane_in, lane_out, limits, x, first, second, *extra)[0]


def residual_body(alpha, parts, x, out, power_out):
    total = parts[0].astype(F32)
    for i in range(1, 32):
        total = total + parts[i].astype(F32)
    low, left = low_rows(), iota((8, 128), 1) < 64
    data = []
    for b in range(8):
        shards = [x[4 * b + n].astype(F32)[56:64] for n in range(4)]
        shards = [shard + pltpu.roll(shard, 64, 1) for shard in shards]
        even, odd = jnp.where(left, shards[0], shards[1]), jnp.where(left, shards[2], shards[3])
        data.append(jnp.where(low, even, swap(odd)))
    u = total - alpha[0] * jnp.concatenate(data, axis=0)
    power = jnp.sum(jnp.sum(u * u, axis=0, keepdims=True), axis=1, keepdims=True)
    power_out[...] = jnp.broadcast_to(power, (8, 128))
    ub = u.astype(BF16)
    for i in range(32):
        out[i] = ub


def powers_body(own, p1, p2, p3, out):
    power = (own[...] + p2[...]) + (p1[...] + p3[...])
    s1 = power.astype(BF16).astype(F32)
    s2 = (power - s1).astype(BF16).astype(F32)
    s3 = power - s1 - s2
    row = iota((8, 128), 0)
    out[...] = jnp.where(row == 0, s1, jnp.where(row == 1, s2, jnp.where(row == 2, s3, 0.0)))


def update_body(ids, parts, direction, out, beta_out, acc):
    acc[...] = jnp.zeros_like(acc)

    def one(i, power):
        part = parts[i].astype(F32)
        for m in range(SLOTS - 1):
            b = ids[i, m]
            acc[b] = acc[b] + part[8 * m : 8 * m + 8]
        return power + part[56:64]

    power = lax.fori_loop(0, 32, one, jnp.zeros((8, 128), F32), unroll=2)
    power = jnp.broadcast_to(jnp.sum(power, axis=0, keepdims=True), (8, 128))
    scale = jnp.sqrt(power / LEFT_COUNT + eps)
    inverse = 1.0 / scale
    beta_out[...] = inverse
    low = low_rows()
    lane = iota((8, 128), 1)
    chunks = [None] * 60
    power = jnp.zeros((8, 128), F32)
    for b in range(30):
        head = acc[b] * inverse - scale * direction[b]
        tail = acc[b + 30] * inverse - scale * direction[b + 30]
        power = power + head * head + tail * tail
        chunks[2 * b] = jnp.where(low, head, swap(tail))
        chunks[2 * b + 1] = jnp.where(low, swap(head), tail)
    power = jnp.sum(jnp.sum(power, axis=0, keepdims=True), axis=1, keepdims=True)
    power = jnp.broadcast_to(power, (8, 128))
    s1 = power.astype(BF16).astype(F32)
    s2 = (power - s1).astype(BF16).astype(F32)
    for j in range(16):
        rows = []
        for q in range(4):
            n, off = 480 * j // 128 + q, 480 * j % 128
            value = chunks[n]
            if off:
                value = pltpu.roll(value, 128 - off, 1)
                if n + 1 < 60:
                    after = pltpu.roll(chunks[n + 1], 128 - off, 1)
                    value = jnp.where(lane < 128 - off, value, after)
            rows.append(value)
        last = jnp.where(lane < 96, rows[3], 0.0)
        last = jnp.where(lane == 120, s1, jnp.where(lane == 121, s2, last))
        rows[3] = jnp.where(lane == 122, power - s1 - s2, last)
        first = [jnp.where(low, rows[q], swap(rows[q + 1])) for q in (0, 2)]
        second = [jnp.where(low, swap(rows[q]), rows[q + 1]) for q in (0, 2)]
        for d, value in ((j, first), (j + 16, second)):
            value = jnp.concatenate(value, axis=0).astype(BF16)
            for g in range(4):
                out[32 * g + d] = value


def halves(x):
    high = x.astype(BF16)
    return high, (x - high.astype(F32)).astype(BF16)


def shrink_body(group, raw, m0, m1, m2, m3, lo, hi, fh, fl, bh, bl, v_next, m_next, wide, back):
    g = group[0]
    for d, part in enumerate((m0, m1, m2, m3)):
        source = lax.rem(g + 4 - d, 4)
        wide[pl.ds(source * 32, 32)] = part[...].astype(F32)
    lane = iota((128, 128), 1)
    count = 2 * WINDOW_FREQS * NVS * RECEIVER_BLOCKS * TILE_EXTENT
    sums = raw[:, 0:16, :].astype(F32)[:, 12, :]
    sums = jnp.where((lane >= 120) & (lane < 123), sums, 0.0)
    power = jnp.sum(jnp.sum(sums, axis=0, keepdims=True), axis=1, keepdims=True)
    inverse = 1.0 / jnp.sqrt(power / count + eps)
    own = raw[pl.ds(g * 32, 32)].astype(F32) * inverse[None]
    for k in range(32):
        for q in range(4):
            width = 128 if q < 3 else 96
            at = slice(128 * q, 128 * q + width)
            v_next[k % 2, k // 2, :, at] = own[k, 4 * q : 4 * q + 4, 0:width]
    wide[...] = wide[...] + raw[...].astype(F32) * inverse[None]
    moment = iota((NT, 128), 0)
    table = jnp.concatenate([fh[...], fl[...]], axis=1)
    at = pl.ds(pl.multiple_of(g * 32, 32), 32)
    own_high, own_low = bh[at], bl[at]
    own_both = jnp.concatenate([own_high, own_low], axis=0)
    for q in range(4):
        inside = (moment >= lo[q : q + 1]) & (moment < hi[q : q + 1])
        inside = jnp.concatenate([inside, inside], axis=1)
        for v in range(0, NVS, 2):
            r = 4 * q + v
            high, low = halves(jnp.concatenate([wide[:, r, :], wide[:, r + 1, :]], axis=1))
            signal = jnp.dot(
                table, jnp.concatenate([high, high], axis=0), preferred_element_type=F32
            ) + jnp.dot(fh[...], low, preferred_element_type=F32)
            kept = signal - jnp.clip(signal, -shrink_level, shrink_level)
            high, low = halves(jnp.where(inside, kept, 0.0))
            result = jnp.dot(own_both, high, preferred_element_type=F32)
            result = result[0:32] + result[32:64]
            result = result + jnp.dot(own_high, low, preferred_element_type=F32)
            back[:, r, :] = result[:, 0:128]
            back[:, r + 1, :] = result[:, 128:256]
    for k in range(32):
        for q in range(4):
            width = 128 if q < 3 else 96
            at = slice(128 * q, 128 * q + width)
            m_next[k % 2, k // 2, :, at] = back[k, 4 * q : 4 * q + 4, 0:width]


def data_body(place, beta, u, u_next):
    inverse = beta[...]
    block, half, odd = place[0] // 4, place[0] // 2 % 2 == 1, place[0] % 2 == 1
    for k in range(32):
        every = u[k].astype(F32)
        part = every[0:8]
        for b in range(1, 8):
            part = jnp.where(block == b, every[8 * b : 8 * b + 8], part)
        part = jnp.where(half, swap(part), part)
        part = jnp.where(odd, pltpu.roll(part, 64, 1), part)
        u_next[k % 2, k // 2] = (part * inverse)[0:4, 0:64]


def transform_tables():
    steps = np.arange(NT)
    bins = FLO + np.arange(WINDOW_FREQS)
    phase = (bins[None, :] * steps[:, None] % NT) * (2.0 * math.pi / NT)
    table = np.stack([np.cos(phase), -np.sin(phase)], axis=2).reshape(NT, 2 * WINDOW_FREQS)
    forward = (table / math.sqrt(WINDOW_FREQS)).astype(np.float32)
    backward = (table.T * (2.0 * math.sqrt(WINDOW_FREQS) / NT)).astype(np.float32)
    out = []
    for a in (forward, backward):
        high = a.astype(ml_dtypes.bfloat16)
        out += [high, (a - high.astype(np.float32)).astype(ml_dtypes.bfloat16)]
    return out


def on_device(
    data_vec,
    direction,
    model,
    alpha,
    u_factor,
    v_factor,
    ranks,
    tile_source_block,
    tile_receiver_block,
    time_lo,
    time_len,
):
    shape = jax.ShapeDtypeStruct
    both = ("freq", "tile")
    g = lax.axis_index("freq")
    place = lax.axis_index("tile")

    def exchange(x, axis):
        return lax.all_to_all(x, axis, split_axis=0, concat_axis=0, tiled=True)

    packed, slots = call(
        pack_body,
        [shape((32, 4, 512), F32), shape((15,), jnp.int32)],
        [SMEM, VMEM],
        [SMEM((64,), jnp.int32), SMEM((SLOTS,), jnp.int32)],
        [VMEM, SMEM],
    )(tile_receiver_block, direction)
    rows = exchange(packed, "tile")
    barrier = lax.optimization_barrier
    lanes = lane_tables(slots, tile_source_block, ranks, data_vec)
    ids = rows[:, 0, 480 : 480 + SLOTS].astype(jnp.int32)
    ids, lanes = barrier((ids, lanes))
    lane_slot, lane_block, limits, data_rows = lanes
    picked, direction_rows = call(
        spread_body,
        [shape((32, 64, 128), BF16), shape((60, 8, 128), F32)],
        [SMEM, VMEM, VMEM],
    )(ids, rows, data_rows)
    x = exchange(picked, "tile")
    model, direction_rows = barrier((model, direction_rows))
    (own_model,) = call(model_body, [shape((32, 16, 128), BF16)], [VMEM])(model)
    models = [own_model] + [
        lax.ppermute(own_model, "freq", [(i, (i + d) % 4) for i in range(4)]) for d in (1, 2, 3)
    ]
    parts = tile_products(lane_slot, lane_block, limits, x, v_factor, u_factor)
    parts, models = barrier((parts, models))
    parts = exchange(parts, "tile")
    residual, power = call(
        residual_body,
        [shape((32, 64, 128), BF16), shape((8, 128), F32)],
        [SMEM, VMEM, VMEM],
    )(alpha.reshape(1), parts, x)
    others = [lax.ppermute(power, "freq", [(i, (i + d) % 4) for i in range(4)]) for d in (1, 2, 3)]
    u_all = exchange(residual, "tile")
    (powers,) = call(powers_body, [shape((8, 128), F32)], [VMEM] * 4)(power, *others)

    back = tile_products(lane_block, lane_slot, limits, u_all, u_factor, v_factor, powers)
    back = exchange(back, "tile")
    raw, beta = call(
        update_body,
        [shape((128, 16, 128), BF16), shape((8, 128), F32)],
        [SMEM, VMEM, VMEM],
        [VMEM((64, 8, 128), F32)],
    )(ids, back, direction_rows)
    raw = exchange(raw, both)

    (u_next,) = call(data_body, [shape(data_vec.shape, F32)], [SMEM, VMEM, VMEM])(
        place.reshape(1), beta, u_all
    )
    lo = jnp.pad(time_lo, (0, 32)).reshape(4, 128)
    hi = jnp.pad(time_lo + time_len, (0, 32)).reshape(4, 128)
    tables = [jnp.asarray(a) for a in transform_tables()]
    v_next, m_next = call(
        shrink_body,
        [shape(direction.shape, F32), shape(direction.shape, F32)],
        [SMEM] + [VMEM] * 11,
        [VMEM((128, 16, 128), F32), VMEM((32, 16, 128), F32)],
    )(g.reshape(1), raw, *models, lo, hi, *tables)
    return u_next, v_next, m_next


def solution(mesh):
    vector = P(None, "freq", None, "tile")
    factor = P("freq", "tile", None, None, None)
    placed = (
        vector,
        vector,
        vector,
        P(),
        factor,
        factor,
        P("freq", "tile"),
        P("tile"),
        P("tile"),
        P("tile"),
        P("tile"),
    )
    return jax.shard_map(
        on_device,
        mesh=mesh,
        in_specs=placed,
        out_specs=(vector, vector, vector),
        check_vma=False,
    )
```

```python
import functools
import math

import jax
import jax.numpy as jnp
import ml_dtypes
import numpy as np
from jax import lax
from jax.experimental import pallas as pl
from jax.experimental.pallas import tpu as pltpu
from jax.sharding import PartitionSpec as P

WINDOW_FREQS = 64
NT = 512
FLO = 8
TILE_EXTENT = 256
RMAX = 48
RECEIVER_BLOCKS = 60
NVS = 4
SLOTS = 8
GROUP = 4
AHEAD = 2
LEFT_COUNT = 2 * WINDOW_FREQS * NVS * 2048

shrink_level = 0.5
eps = 1e-06

F32 = jnp.float32
BF16 = jnp.bfloat16
VMEM = pltpu.VMEM
SMEM = pltpu.SMEM
LIMIT = 16 * 1024 * 1024
TILES_LIMIT = 50 * 1024 * 1024


def iota(shape, axis):
    return lax.broadcasted_iota(jnp.int32, shape, axis)


def low_rows():
    return iota((8, 128), 0) < 4


def swap(x):
    return pltpu.roll(x, 4, 0)


def call(body, outs, ins, scratch=(), out_spaces=None, limit=LIMIT):
    out_spaces = out_spaces or [VMEM] * len(outs)
    return pl.pallas_call(
        body,
        out_shape=outs,
        in_specs=[pl.BlockSpec(memory_space=s) for s in ins],
        out_specs=[pl.BlockSpec(memory_space=s) for s in out_spaces],
        scratch_shapes=list(scratch),
        compiler_params=pltpu.CompilerParams(vmem_limit_bytes=limit),
    )


def pack_body(rb, direction, out, slot_of):
    blocks = [rb[t] for t in range(rb.shape[0])]
    lane = iota((4, 128), 1)
    listed = jnp.zeros((4, 128), F32)
    slots = []
    count = jnp.int32(0)
    for t, b in enumerate(blocks):
        slot = count
        for earlier, at in zip(blocks[:t], slots):
            slot = jnp.where(b == earlier, at, slot)
        slots.append(slot)
        slot_of[t] = slot
        count = jnp.maximum(count, slot + 1)
        listed = jnp.where(lane == 96 + slot, b.astype(F32), listed)
    for f in range(direction.shape[1]):
        for c in range(2):
            k = 2 * f + c
            out[k, :, 384:512] = listed
            out[k, :, 0:480] = direction[c, f]


def model_body(model, out):
    for f in range(model.shape[1]):
        for c in range(2):
            rows = [model[c, f, :, 128 * q : 128 * q + 128] for q in range(3)]
            rows.append(jnp.concatenate([model[c, f, :, 384:480], jnp.zeros((4, 32), F32)], axis=1))
            out[2 * f + c] = jnp.concatenate(rows, axis=0).astype(BF16)


def blocks_of(chunks, half):
    low = low_rows()
    blocks = [None] * (2 * half)
    for b in range(half):
        even, odd = chunks[2 * b], chunks[2 * b + 1]
        blocks[b] = jnp.where(low, even, swap(odd))
        blocks[b + half] = jnp.where(low, swap(even), odd)
    return blocks


def spread_body(ids, rows, data, out, direction):
    lane = iota((8, 512), 1)
    chunks = [None] * 60
    empty = jnp.zeros((8, 128), F32)
    for j in range(16):
        both = jnp.concatenate([rows[j], rows[j + 16]], axis=0)
        shift, first = 480 * j % 128, 480 * j // 128
        moved = jnp.concatenate([jnp.where(lane < 480, both, 0.0), empty], axis=1)
        if shift:
            moved = pltpu.roll(moved, shift, 1)
        for q in range((shift + 479) // 128 + 1):
            piece = moved[:, 128 * q : 128 * q + 128]
            n = first + q
            chunks[n] = piece if chunks[n] is None else chunks[n] + piece
    for b, block in enumerate(blocks_of(chunks, 30)):
        direction[b] = block

    def one(i, _):
        picked = [direction[ids[i, m]] for m in range(SLOTS - 1)]
        picked.append(data[i])
        out[i] = jnp.concatenate(picked, axis=0).astype(BF16)
        return 0

    lax.fori_loop(0, 32, one, 0, unroll=4)


def lanes_body(slots, blocks, ranks, data, lane_slot, lane_block, limit, data_rows):
    tiles = ranks.shape[1]
    wide = RMAX * tiles
    lane = iota((8, wide), 1)
    for ref, out in ((slots, lane_slot), (blocks, lane_block)):
        value = jnp.full((8, wide), ref[0], jnp.int32)
        for t in range(1, tiles):
            value = jnp.where(lane >= RMAX * t, ref[t], value)
        out[...] = value
    tile, lane = iota((tiles, wide), 0), iota((tiles, wide), 1)
    within = lane - RMAX * tile
    spread = jnp.where((within >= 0) & (within < RMAX), 1.0, 0.0).astype(BF16)
    rank = jnp.dot(ranks[...].astype(F32).astype(BF16), spread, preferred_element_type=F32)
    start = jnp.zeros((1, wide), jnp.int32)
    lane = iota((1, wide), 1)
    for t in range(1, tiles):
        start = jnp.where(lane >= RMAX * t, RMAX * t, start)
    limit[...] = rank.astype(jnp.int32) + start
    for k in range(32):
        own = data[k % 2, k // 2]
        high = own.astype(BF16).astype(F32)
        own = jnp.concatenate([high, own - high], axis=1)
        data_rows[k] = jnp.concatenate([own, jnp.zeros((4, 128), F32)], axis=0)


def tiles_body(extra, lane_in, lane_out, limits, x, first_hbm, second_hbm, *refs):
    rest, (out, first, second, sems) = refs[:-4], refs[-4:]
    steps = first.shape[0] // GROUP

    def copies(n):
        span = pl.ds(n * GROUP, GROUP)
        return [
            pltpu.make_async_copy(source.at[span], target.at[span], sems.at[a, n])
            for a, (source, target) in enumerate(((first_hbm, first), (second_hbm, second)))
        ]

    for n in range(AHEAD):
        for copy in copies(n):
            copy.start()
    tiles = first.shape[1]
    wide = RMAX * tiles
    low = low_rows()
    turned = (((1,), (1,)), ((), ()))
    source, target = lane_in[...], lane_out[...]
    lane = iota((8, wide), 1)
    upper = iota((8, wide), 0) < 4

    def one(f):
        xr = x[2 * f, 0:64].astype(F32)
        xi = x[2 * f + 1, 0:64].astype(F32)
        real, imag = [], []
        for m in range(SLOTS):
            tr = xr[8 * m : 8 * m + 8]
            ti = xi[8 * m : 8 * m + 8]
            tr4, ti4 = swap(tr), swap(ti)
            real.append(jnp.concatenate([jnp.where(low, tr, ti4), jnp.where(low, tr4, ti)], axis=1))
            imag.append(
                jnp.concatenate([jnp.where(low, ti, -tr4), jnp.where(low, ti4, -tr)], axis=1)
            )
        real = jnp.concatenate(real, axis=0).astype(BF16)
        imag = jnp.concatenate(imag, axis=0).astype(BF16)
        every = lax.dot_general(
            real, first[f, :, 0].reshape(wide, TILE_EXTENT), turned, preferred_element_type=F32
        ) + lax.dot_general(
            imag, first[f, :, 1].reshape(wide, TILE_EXTENT), turned, preferred_element_type=F32
        )
        z = every[0:8]
        for m in range(1, SLOTS):
            z = jnp.where(source == m, every[8 * m : 8 * m + 8], z)
        z = jnp.where(lane < limits[pl.ds(f, 1)], z, 0.0)
        turn = pltpu.roll(z, 4, 0)
        turn = jnp.where(upper, -turn, turn)
        za = [jnp.where(target == m, z, 0.0) for m in range(SLOTS)]
        zb = [jnp.where(target == m, turn, 0.0) for m in range(SLOTS)]
        za = jnp.concatenate(za, axis=0).astype(BF16)
        zb = jnp.concatenate(zb, axis=0).astype(BF16)
        c = jnp.dot(
            za, second[f, :, 0].reshape(wide, TILE_EXTENT), preferred_element_type=F32
        ) + jnp.dot(zb, second[f, :, 1].reshape(wide, TILE_EXTENT), preferred_element_type=F32)
        real, imag = [], []
        for m in range(SLOTS):
            left, right = c[8 * m : 8 * m + 8, 0:128], c[8 * m : 8 * m + 8, 128:256]
            real.append(jnp.where(low, left, swap(right)))
            imag.append(jnp.where(low, swap(left), right))
        if extra:
            real[-1] = imag[-1] = rest[0][...]
        out[2 * f] = jnp.concatenate(real, axis=0).astype(out.dtype)
        out[2 * f + 1] = jnp.concatenate(imag, axis=0).astype(out.dtype)

    def group(n, _):
        for copy in copies(n):
            copy.wait()

        @pl.when(n + AHEAD < steps)
        def _():
            for copy in copies(n + AHEAD):
                copy.start()

        for f in range(GROUP):
            one(n * GROUP + f)
        return 0

    lax.fori_loop(0, steps, group, 0)


def lane_tables(slots, blocks, ranks, data):
    wide = RMAX * ranks.shape[1]
    table = jax.ShapeDtypeStruct((8, wide), jnp.int32)
    limit = jax.ShapeDtypeStruct((ranks.shape[0], wide), jnp.int32)
    rows = jax.ShapeDtypeStruct((32, 8, 128), F32)
    return call(lanes_body, [table, table, limit, rows], [SMEM, SMEM, VMEM, VMEM])(
        slots, blocks, ranks, data
    )


def tile_products(lane_in, lane_out, limits, x, first, second, *extra):
    return call(
        functools.partial(tiles_body, bool(extra)),
        [jax.ShapeDtypeStruct((2 * first.shape[0], 64, 128), BF16)],
        [VMEM] * 4 + [pltpu.HBM] * 2 + [VMEM] * len(extra),
        [
            VMEM(first.shape, BF16),
            VMEM(second.shape, BF16),
            pltpu.SemaphoreType.DMA((2, first.shape[0] // GROUP)),
        ],
        limit=TILES_LIMIT,
    )(lane_in, lane_out, limits, x, first, second, *extra)[0]


def residual_body(alpha, parts, x, out, power_out):
    total = parts[0].astype(F32)
    for i in range(1, 32):
        total = total + parts[i].astype(F32)
    low, left = low_rows(), iota((8, 128), 1) < 64
    data = []
    for b in range(8):
        shards = [x[4 * b + n].astype(F32)[56:64] for n in range(4)]
        shards = [shard + pltpu.roll(shard, 64, 1) for shard in shards]
        even, odd = jnp.where(left, shards[0], shards[1]), jnp.where(left, shards[2], shards[3])
        data.append(jnp.where(low, even, swap(odd)))
    u = total - alpha[0] * jnp.concatenate(data, axis=0)
    power = jnp.sum(jnp.sum(u * u, axis=0, keepdims=True), axis=1, keepdims=True)
    power_out[...] = jnp.broadcast_to(power, (8, 128))
    ub = u.astype(BF16)
    for i in range(32):
        out[i] = ub


def powers_body(own, p1, p2, p3, out):
    power = (own[...] + p2[...]) + (p1[...] + p3[...])
    s1 = power.astype(BF16).astype(F32)
    s2 = (power - s1).astype(BF16).astype(F32)
    s3 = power - s1 - s2
    row = iota((8, 128), 0)
    out[...] = jnp.where(row == 0, s1, jnp.where(row == 1, s2, jnp.where(row == 2, s3, 0.0)))


def update_body(ids, parts, direction, out, beta_out, acc):
    acc[...] = jnp.zeros_like(acc)

    def one(i, power):
        part = parts[i].astype(F32)
        for m in range(SLOTS - 1):
            b = ids[i, m]
            acc[b] = acc[b] + part[8 * m : 8 * m + 8]
        return power + part[56:64]

    power = lax.fori_loop(0, 32, one, jnp.zeros((8, 128), F32), unroll=2)
    power = jnp.broadcast_to(jnp.sum(power, axis=0, keepdims=True), (8, 128))
    scale = jnp.sqrt(power / LEFT_COUNT + eps)
    inverse = 1.0 / scale
    beta_out[...] = inverse
    low = low_rows()
    lane = iota((8, 128), 1)
    chunks = [None] * 60
    power = jnp.zeros((8, 128), F32)
    for b in range(30):
        head = acc[b] * inverse - scale * direction[b]
        tail = acc[b + 30] * inverse - scale * direction[b + 30]
        power = power + head * head + tail * tail
        chunks[2 * b] = jnp.where(low, head, swap(tail))
        chunks[2 * b + 1] = jnp.where(low, swap(head), tail)
    power = jnp.sum(jnp.sum(power, axis=0, keepdims=True), axis=1, keepdims=True)
    power = jnp.broadcast_to(power, (8, 128))
    s1 = power.astype(BF16).astype(F32)
    s2 = (power - s1).astype(BF16).astype(F32)
    for j in range(16):
        rows = []
        for q in range(4):
            n, off = 480 * j // 128 + q, 480 * j % 128
            value = chunks[n]
            if off:
                value = pltpu.roll(value, 128 - off, 1)
                if n + 1 < 60:
                    after = pltpu.roll(chunks[n + 1], 128 - off, 1)
                    value = jnp.where(lane < 128 - off, value, after)
            rows.append(value)
        last = jnp.where(lane < 96, rows[3], 0.0)
        last = jnp.where(lane == 120, s1, jnp.where(lane == 121, s2, last))
        rows[3] = jnp.where(lane == 122, power - s1 - s2, last)
        first = [jnp.where(low, rows[q], swap(rows[q + 1])) for q in (0, 2)]
        second = [jnp.where(low, swap(rows[q]), rows[q + 1]) for q in (0, 2)]
        for d, value in ((j, first), (j + 16, second)):
            value = jnp.concatenate(value, axis=0).astype(BF16)
            for g in range(4):
                out[32 * g + d] = value


def halves(x):
    high = x.astype(BF16)
    return high, (x - high.astype(F32)).astype(BF16)


def shrink_body(group, raw, m0, m1, m2, m3, lo, hi, fh, fl, bh, bl, v_next, m_next, wide, back):
    g = group[0]
    for d, part in enumerate((m0, m1, m2, m3)):
        source = lax.rem(g + 4 - d, 4)
        wide[pl.ds(source * 32, 32)] = part[...].astype(F32)
    lane = iota((128, 128), 1)
    count = 2 * WINDOW_FREQS * NVS * RECEIVER_BLOCKS * TILE_EXTENT
    sums = raw[:, 0:16, :].astype(F32)[:, 12, :]
    sums = jnp.where((lane >= 120) & (lane < 123), sums, 0.0)
    power = jnp.sum(jnp.sum(sums, axis=0, keepdims=True), axis=1, keepdims=True)
    inverse = 1.0 / jnp.sqrt(power / count + eps)
    own = raw[pl.ds(g * 32, 32)].astype(F32) * inverse[None]
    for k in range(32):
        for q in range(4):
            width = 128 if q < 3 else 96
            at = slice(128 * q, 128 * q + width)
            v_next[k % 2, k // 2, :, at] = own[k, 4 * q : 4 * q + 4, 0:width]
    wide[...] = wide[...] + raw[...].astype(F32) * inverse[None]
    moment = iota((NT, 128), 0)
    table = jnp.concatenate([fh[...], fl[...]], axis=1)
    at = pl.ds(pl.multiple_of(g * 32, 32), 32)
    own_high, own_low = bh[at], bl[at]
    own_both = jnp.concatenate([own_high, own_low], axis=0)
    for q in range(4):
        inside = (moment >= lo[q : q + 1]) & (moment < hi[q : q + 1])
        inside = jnp.concatenate([inside, inside], axis=1)
        for v in range(0, NVS, 2):
            r = 4 * q + v
            high, low = halves(jnp.concatenate([wide[:, r, :], wide[:, r + 1, :]], axis=1))
            signal = jnp.dot(
                table, jnp.concatenate([high, high], axis=0), preferred_element_type=F32
            ) + jnp.dot(fh[...], low, preferred_element_type=F32)
            kept = signal - jnp.clip(signal, -shrink_level, shrink_level)
            high, low = halves(jnp.where(inside, kept, 0.0))
            result = jnp.dot(own_both, high, preferred_element_type=F32)
            result = result[0:32] + result[32:64]
            result = result + jnp.dot(own_high, low, preferred_element_type=F32)
            back[:, r, :] = result[:, 0:128]
            back[:, r + 1, :] = result[:, 128:256]
    for k in range(32):
        for q in range(4):
            width = 128 if q < 3 else 96
            at = slice(128 * q, 128 * q + width)
            m_next[k % 2, k // 2, :, at] = back[k, 4 * q : 4 * q + 4, 0:width]


def data_body(place, beta, u, u_next):
    inverse = beta[...]
    block, half, odd = place[0] // 4, place[0] // 2 % 2 == 1, place[0] % 2 == 1
    for k in range(32):
        every = u[k].astype(F32)
        part = every[0:8]
        for b in range(1, 8):
            part = jnp.where(block == b, every[8 * b : 8 * b + 8], part)
        part = jnp.where(half, swap(part), part)
        part = jnp.where(odd, pltpu.roll(part, 64, 1), part)
        u_next[k % 2, k // 2] = (part * inverse)[0:4, 0:64]


def transform_tables():
    steps = np.arange(NT)
    bins = FLO + np.arange(WINDOW_FREQS)
    phase = (bins[None, :] * steps[:, None] % NT) * (2.0 * math.pi / NT)
    table = np.stack([np.cos(phase), -np.sin(phase)], axis=2).reshape(NT, 2 * WINDOW_FREQS)
    forward = (table / math.sqrt(WINDOW_FREQS)).astype(np.float32)
    backward = (table.T * (2.0 * math.sqrt(WINDOW_FREQS) / NT)).astype(np.float32)
    out = []
    for a in (forward, backward):
        high = a.astype(ml_dtypes.bfloat16)
        out += [high, (a - high.astype(np.float32)).astype(ml_dtypes.bfloat16)]
    return out


def on_device(
    data_vec,
    direction,
    model,
    alpha,
    u_factor,
    v_factor,
    ranks,
    tile_source_block,
    tile_receiver_block,
    time_lo,
    time_len,
):
    shape = jax.ShapeDtypeStruct
    both = ("freq", "tile")
    g = lax.axis_index("freq")
    place = lax.axis_index("tile")

    def exchange(x, axis):
        return lax.all_to_all(x, axis, split_axis=0, concat_axis=0, tiled=True)

    packed, slots = call(
        pack_body,
        [shape((32, 4, 512), F32), shape((15,), jnp.int32)],
        [SMEM, VMEM],
        (),
        [VMEM, SMEM],
    )(tile_receiver_block, direction)
    rows = exchange(packed, "tile")
    barrier = lax.optimization_barrier
    lanes = lane_tables(slots, tile_source_block, ranks, data_vec)
    ids = rows[:, 0, 480 : 480 + SLOTS].astype(jnp.int32)
    ids, lanes = barrier((ids, lanes))
    lane_slot, lane_block, limits, data_rows = lanes
    picked, direction_rows = call(
        spread_body,
        [shape((32, 64, 128), BF16), shape((60, 8, 128), F32)],
        [SMEM, VMEM, VMEM],
    )(ids, rows, data_rows)
    x = exchange(picked, "tile")
    model, direction_rows = barrier((model, direction_rows))
    (own_model,) = call(model_body, [shape((32, 16, 128), BF16)], [VMEM])(model)
    models = [own_model] + [
        lax.ppermute(own_model, "freq", [(i, (i + d) % 4) for i in range(4)]) for d in (1, 2, 3)
    ]
    parts = tile_products(lane_slot, lane_block, limits, x, v_factor, u_factor)
    parts, models = barrier((parts, models))
    parts = exchange(parts, "tile")
    residual, power = call(
        residual_body,
        [shape((32, 64, 128), BF16), shape((8, 128), F32)],
        [SMEM, VMEM, VMEM],
    )(alpha.reshape(1), parts, x)
    others = [lax.ppermute(power, "freq", [(i, (i + d) % 4) for i in range(4)]) for d in (1, 2, 3)]
    u_all = exchange(residual, "tile")
    (powers,) = call(powers_body, [shape((8, 128), F32)], [VMEM] * 4)(power, *others)

    back = tile_products(lane_block, lane_slot, limits, u_all, u_factor, v_factor, powers)
    back = exchange(back, "tile")
    raw, beta = call(
        update_body,
        [shape((128, 16, 128), BF16), shape((8, 128), F32)],
        [SMEM, VMEM, VMEM],
        [VMEM((64, 8, 128), F32)],
    )(ids, back, direction_rows)
    raw = exchange(raw, both)

    (u_next,) = call(data_body, [shape(data_vec.shape, F32)], [SMEM, VMEM, VMEM])(
        place.reshape(1), beta, u_all
    )
    lo = jnp.pad(time_lo, (0, 32)).reshape(4, 128)
    hi = jnp.pad(time_lo + time_len, (0, 32)).reshape(4, 128)
    tables = [jnp.asarray(a) for a in transform_tables()]
    v_next, m_next = call(
        shrink_body,
        [shape(direction.shape, F32), shape(direction.shape, F32)],
        [SMEM] + [VMEM] * 11,
        [VMEM((128, 16, 128), F32), VMEM((32, 16, 128), F32)],
    )(g.reshape(1), raw, *models, lo, hi, *tables)
    return u_next, v_next, m_next


def solution(mesh):
    vector = P(None, "freq", None, "tile")
    factor = P("freq", "tile", None, None, None)
    placed = (
        vector,
        vector,
        vector,
        P(),
        factor,
        factor,
        P("freq", "tile"),
        P("tile"),
        P("tile"),
        P("tile"),
        P("tile"),
    )
    return jax.shard_map(
        on_device,
        mesh=mesh,
        in_specs=placed,
        out_specs=(vector, vector, vector),
        check_vma=False,
    )
```
